256 devices in a mesh: dp: 32 (over y, z), seq: 8 (over x, core).
Axes of the slice: x: 4, y: 4, z: 8, core: 2. Of those that a mesh axis runs over, the one named last changes fastest.
Arguments:
- q_in: bfloat16 [32768, 3072], P(('dp', 'seq')), may hold values from -6 to 6
- k_in: bfloat16 [32768, 3072], P(('dp', 'seq')), may hold values from -6 to 6
- v_in: bfloat16 [32768, 3072], P(('dp', 'seq')), may hold values from -6 to 6
- q_gain: float32 [128], replicated, may hold values from 0.6 to 5
- k_gain: float32 [128], replicated, may hold values from 0.6 to 5
- image_tokens: int32 [64], replicated, may hold values from 192 to 576, as said below
- text_tokens: int32 [64], replicated, may hold values from 1 to 128
Outputs:
- attended: bfloat16 [32768, 3072], P(('dp', 'seq'))
The draws below stay inside these ranges and needn't reach their ends.
Inputs may be any that keep to these rules, and one draw needn't show every extreme that they name: The samples fill the pack exactly: the image_tokens sum to 24576.
All inputs are finite; a program needn't handle non-finite values.
Results may differ from the reference program's by a relative error of at most 0.012.
The reference program's roundings to bfloat16 on the way (of `q_norm`, `k_norm` and `probs`) count: a program that leaves them out, or rounds other values in their place, can miss the bound.
Values may be sent and summed in bfloat16 or wider, within the bound.
A program may use at most 64 MiB of HBM per device.

```python
import jax
import jax.numpy as jnp
from jax import lax

HD = 128
TXT = 128
TOK_DEV = 128
HW = 3072
TOKENS = 32768
SAMPLES = 64
MEANL = 384
SPREAD = 192
RIM = 703
N_SEQ = 8


def shared_keys(key):
    return jnp.clip(jax.random.normal(key, (TOKENS, HW), jnp.float32), -6.0, 6.0)


def draw_k_in(key, part):
    return shared_keys(key).astype(jnp.bfloat16)


def draw_q_in(key, part):
    key = jax.random.fold_in(key, 11)
    first = jax.random.fold_in(key, 0)
    mixed = jnp.clip(jax.random.normal(first, (TOKENS, HW), jnp.float32), -6.0, 6.0)
    return mixed.astype(jnp.bfloat16)


def gain_values(key, lower, upper):
    spread = jax.random.uniform(key, (HD,), jnp.float32, jnp.log(lower), jnp.log(upper))
    return jnp.exp(spread)


def draw_q_gain(key, part):
    key = jax.random.fold_in(key, 21)
    return gain_values(key, 0.6, 2.5)


def draw_k_gain(key, part):
    key = jax.random.fold_in(key, 22)
    return gain_values(key, 0.6, 2.5)


def draw_image_tokens(key, part):
    key = jax.random.fold_in(key, 5)
    first, second, third = jax.random.split(key, 3)
    pairs = SAMPLES // 2
    swing = jax.random.randint(first, (pairs,), -SPREAD, SPREAD + 1)
    forced = jax.random.randint(second, (), 0, pairs)
    swing = jnp.where(jnp.arange(pairs) == forced, SPREAD, swing)
    lengths = jnp.concatenate((MEANL + swing, MEANL - swing))
    order = jax.random.permutation(third, SAMPLES)
    return lengths[order].astype(jnp.int32)


def touch_ends(values, stream_key, low, high):
    place = [jax.random.randint(jax.random.fold_in(stream_key, axis), (), 0, length) for axis, length in enumerate(values.shape)]
    main_axis = values.shape.index(max(values.shape))
    next_to = place[:main_axis] + [(place[main_axis] + 1) % values.shape[main_axis]] + place[main_axis + 1:]
    return values.at[tuple(place)].set(low).at[tuple(next_to)].set(high)


def steps_of(own_key, dims, cuts, low, high):
    factor_of, own = 1.0, jax.random.fold_in(own_key, 6)
    for position, shards_of in cuts:
        heights = jnp.exp(jax.random.uniform(jax.random.fold_in(own, position), (shards_of,), jnp.float32, low / len(cuts), high / len(cuts)))
        factor_of = factor_of * jnp.repeat(heights, dims[position] // shards_of).reshape([-1 if axis == position else 1 for axis in range(len(dims))])
    return factor_of


def scatter_about(own_key, dims, scale, most, shards=(), held_as=jnp.bfloat16):
    array = scale * jax.random.normal(own_key, dims, jnp.float32)
    if shards:
        array = array * steps_of(own_key, dims, shards, -0.22, 0.18)
    return jnp.clip(array, -most, most).astype(held_as)


def setup_inputs(seed: int = 0) -> dict:
    key_of = jax.random.split(jax.random.key(seed), 8)
    return {
        "q_in": draw_q_in(jax.random.fold_in(key_of[7], 71), 0),
        "k_in": draw_k_in(jax.random.fold_in(key_of[7], 71), 0),
        "v_in": scatter_about(key_of[2], (TOKENS, HW), 1.0, 6.0, ((0, 256),)),
        "q_gain": draw_q_gain(jax.random.fold_in(key_of[7], 71), 0),
        "k_gain": draw_k_gain(jax.random.fold_in(key_of[7], 71), 0),
        "image_tokens": draw_image_tokens(jax.random.fold_in(key_of[7], 71), 0),
        "text_tokens": touch_ends(jax.random.randint(key_of[6], (SAMPLES,), 1, TXT + 1), jax.random.fold_in(key_of[6], 1), 1, TXT).astype(jnp.int32),
    }


EPS = 1e-06

def qk_norm(values, gain):
    rows = values.shape[0]
    shaped = values.astype(jnp.float32).reshape(rows, -1, HD)
    square = lax.optimization_barrier(jnp.mean(shaped * shaped, axis=-1, keepdims=True))
    return (shaped * lax.rsqrt(square + EPS) * gain).reshape(rows, -1).astype(jnp.bfloat16)

def layout(image_tokens, text_tokens, positions):
    lengths = TXT + image_tokens
    ends = jnp.cumsum(lengths).astype(jnp.int32)
    starts = ends - lengths
    inside = (positions >= 0) & (positions < ends[-1])
    owner = lax.optimization_barrier(jnp.sum((positions[:, None] >= ends[None, :]).astype(jnp.int32), axis=1))
    match = owner[:, None] == jnp.arange(lengths.shape[0], dtype=jnp.int32)[None, :]
    first = lax.optimization_barrier(jnp.sum(jnp.where(match, starts[None, :], 0), axis=1))
    count = lax.optimization_barrier(jnp.sum(jnp.where(match, text_tokens[None, :], 0), axis=1))
    offset = positions - first
    usable = inside & ((offset >= TXT) | (offset < count))
    owner = jnp.where(inside, owner, -1)
    return (owner, usable)

def attend(q_rows, k_rows, v_rows, q_owner, k_owner, k_usable):
    rows = q_rows.shape[0]
    heads = q_rows.shape[1] // HD
    q_heads = q_rows.astype(jnp.float32).reshape(rows, heads, HD)
    k_heads = k_rows.astype(jnp.float32).reshape(k_rows.shape[0], heads, HD)
    v_heads = v_rows.astype(jnp.float32).reshape(v_rows.shape[0], heads, HD)
    scores = jnp.einsum('qhd,khd->hqk', q_heads, k_heads) * (1.0 / HD ** 0.5)
    allowed = (q_owner[:, None] == k_owner[None, :]) & k_usable[None, :]
    scores = jnp.where(allowed[None], scores, -1e+30)
    top = lax.optimization_barrier(jnp.max(scores, axis=-1, keepdims=True))
    weights = jnp.where(allowed[None], jnp.exp(scores - top), 0.0)
    total = lax.optimization_barrier(jnp.sum(weights, axis=-1, keepdims=True))
    probs = (weights / total).astype(jnp.bfloat16).astype(jnp.float32)
    result = jnp.einsum('hqk,khd->qhd', probs, v_heads)
    return result.reshape(rows, heads * HD).astype(jnp.bfloat16)

def reference(q_in, k_in, v_in, q_gain, k_gain, image_tokens, text_tokens):
    block = min(512, TOK_DEV * N_SEQ)
    q_norm = qk_norm(q_in, q_gain)
    k_norm = qk_norm(k_in, k_gain)
    k_padded = jnp.pad(k_norm, ((RIM, RIM), (0, 0)))
    v_padded = jnp.pad(v_in, ((RIM, RIM), (0, 0)))
    q_owner, q_usable = layout(image_tokens, text_tokens, jnp.arange(TOKENS, dtype=jnp.int32))
    k_owner, k_usable = layout(image_tokens, text_tokens, jnp.arange(TOKENS + 2 * RIM, dtype=jnp.int32) - RIM)

    def one_block(index):
        start = (index * block).astype(jnp.int32)
        span = block + 2 * RIM
        return attend(lax.dynamic_slice_in_dim(q_norm, start, block, 0), lax.dynamic_slice_in_dim(k_padded, start, span, 0), lax.dynamic_slice_in_dim(v_padded, start, span, 0), lax.dynamic_slice_in_dim(q_owner, start, block, 0), lax.dynamic_slice_in_dim(k_owner, start, span, 0), lax.dynamic_slice_in_dim(k_usable, start, span, 0))
    blocks = lax.map(one_block, jnp.arange(TOKENS // block, dtype=jnp.int32))
    return blocks.reshape(TOKENS, HW)
```

```python
import functools

import jax
import jax.numpy as jnp
from jax import lax
from jax.experimental import pallas as pl
from jax.experimental.pallas import tpu as pltpu
from jax.sharding import PartitionSpec as P

MESH = pl.DeviceIdType.MESH
BF16 = jnp.bfloat16
F32 = jnp.float32

HD = 128
TXT = 128
EPS = 1e-06
SEQ = 8
SLOTS = 3
ROWS = 128
GROUP = SEQ * ROWS
HALO = 704
EXT = GROUP + 2 * HALO
BLOCK = 256
WINDOW = BLOCK + 2 * HALO
SAMPLES = 64

MARK_Q = 64.0
MARK_K = 128.0
SCALE = 1.4426950408889634 / HD**0.5

OTHERS = ((1, 0), (1, 1), (-1, 0), (-1, 1), (2, 0), (2, 1), (0, 1))
ARRIVAL = ((0, 0), (0, 1), (1, 0), (-1, 0), (1, 1), (-1, 1), (2, 0), (2, 1))
NT = (((1,), (1,)), ((), ()))


def partner(s, dx, dc):
    return lax.rem(s // 2 + dx + 4, 4) * 2 + lax.rem(s % 2 + dc, 2)


def kernel(
    groups,
    q_in, k_in, v_in, q_gain, k_gain, image, text,
    out,
    q_buf, k_buf, v_buf, kv_src, q_src, kv, q_all, o_buf, mark_q, mark_k, ints,
    load_sem, own_sem, kv_send, kv_recv, q_send, q_recv,
    left_send, left_recv, right_send, right_recv, out_send, out_recv, out_own,
):
    dp = lax.axis_index("dp")
    s = lax.axis_index("seq")
    after = lax.rem(dp + 1, groups)
    before = lax.rem(dp + groups - 1, groups)

    barrier = pltpu.get_barrier_semaphore()
    for dx, dc in OTHERS:
        pl.semaphore_signal(barrier, 1, device_id=(dp, partner(s, dx, dc)), device_id_type=MESH)
    pl.semaphore_signal(barrier, 1, device_id=(after, s), device_id_type=MESH)
    pl.semaphore_signal(barrier, 1, device_id=(before, s), device_id_type=MESH)

    loads = [
        pltpu.make_async_copy(src, dst, load_sem.at[i])
        for i, (src, dst) in enumerate(((k_in, k_buf), (v_in, v_buf), (q_in, q_buf)))
    ]
    for load in loads:
        load.start()

    def cols(head):
        return pl.ds(pl.multiple_of(head * HD, HD), HD)

    def normed(buf, head, gain):
        x = buf[:, cols(head)].astype(F32)
        square = jnp.sum(x * x, axis=1, keepdims=True) * (1.0 / HD)
        return (x * lax.rsqrt(square + EPS) * gain[...]).astype(BF16)

    def remote(src, dst, send, recv, dev):
        return pltpu.make_async_remote_copy(
            src_ref=src, dst_ref=dst, send_sem=send, recv_sem=recv, device_id=dev, device_id_type=MESH
        )

    def kv_rows(j, first, count):
        return kv.at[j, :, pl.ds(pl.multiple_of(first, 64), count), :]

    def kv_copy(j, to, source, index):
        return remote(
            kv_src.at[to * SLOTS + j], kv_rows(j, HALO + source * ROWS, ROWS),
            kv_send.at[j, index], kv_recv.at[j, source], (dp, to),
        )

    def q_copy(j, to, source, index):
        return remote(
            q_src.at[to * SLOTS + j], q_all.at[j, pl.ds(pl.multiple_of(source * ROWS, ROWS), ROWS), :],
            q_send.at[j, index], q_recv.at[j, source], (dp, to),
        )

    def left_copy(j, source, skip):
        first = source * ROWS + skip
        return remote(
            kv_rows(j, HALO + first, ROWS - skip), kv_rows(j, first - (GROUP - HALO), ROWS - skip),
            left_send.at[j, source], left_recv.at[j, source], (after, s),
        )

    def right_copy(j, source, count):
        first = source * ROWS
        return remote(
            kv_rows(j, HALO + first, count), kv_rows(j, HALO + GROUP + first, count),
            right_send.at[j, source], right_recv.at[j, source], (before, s),
        )

    def out_copy(j, to, source):
        return remote(
            o_buf.at[j, pl.ds(pl.multiple_of(to * ROWS, ROWS), ROWS), :], out.at[:, cols(source * SLOTS + j)],
            out_send.at[j, to], out_recv.at[j, source], (dp, to),
        )

    def own_kv(j):
        return pltpu.make_async_copy(kv_src.at[s * SLOTS + j], kv_rows(j, HALO + s * ROWS, ROWS), own_sem.at[0, j])

    def own_q(j):
        return pltpu.make_async_copy(
            q_src.at[s * SLOTS + j], q_all.at[j, pl.ds(pl.multiple_of(s * ROWS, ROWS), ROWS), :], own_sem.at[1, j]
        )

    def own_out(j):
        return pltpu.make_async_copy(
            o_buf.at[j, pl.ds(pl.multiple_of(s * ROWS, ROWS), ROWS), :], out.at[:, cols(s * SLOTS + j)], out_own.at[j]
        )

    def send_kv(j):
        for index, (dx, dc) in enumerate(OTHERS):
            kv_copy(j, partner(s, dx, dc), s, index).start()

    def send_q(j):
        for index, (dx, dc) in enumerate(OTHERS):
            q_copy(j, partner(s, dx, dc), s, index).start()

    def pass_on(j):
        for dx, dc in ARRIVAL:
            source = partner(s, dx, dc)
            if (dx, dc) == (0, 0):
                own_kv(j).wait()
            else:
                kv_copy(j, s, source, 0).wait_recv()

            @pl.when(source >= 3)
            def _():
                left_copy(j, source, 0).start()

            @pl.when(source == 2)
            def _():
                left_copy(j, source, 64).start()

            @pl.when(source <= 4)
            def _():
                right_copy(j, source, ROWS).start()

            @pl.when(source == 5)
            def _():
                right_copy(j, source, 64).start()

    def attend(j):
        for dx, dc in OTHERS:
            q_copy(j, s, partner(s, dx, dc), 0).wait_recv()
        own_q(j).wait()
        for source in range(2, SEQ):
            left_copy(j, source, 64 if source == 2 else 0).wait_recv()
        for source in range(6):
            right_copy(j, source, 64 if source == 5 else ROWS).wait_recv()
        for i in range(GROUP // BLOCK):
            rows, window = pl.ds(i * BLOCK, BLOCK), pl.ds(i * BLOCK, WINDOW)
            q = jnp.concatenate([q_all[j, rows, :], mark_q[rows, :]], axis=1)
            k = jnp.concatenate([kv[j, 0, window, :], mark_k[window, :]], axis=1)
            v = kv[j, 1, window, :]
            scores = lax.dot_general(q, k, NT, preferred_element_type=F32)
            top = jnp.max(scores, axis=1, keepdims=True)
            weights = jnp.exp2((scores - top) * SCALE).astype(BF16)
            sums = jnp.dot(weights, jnp.concatenate([v, jnp.ones_like(v)], axis=1), preferred_element_type=F32)
            o_buf[j, rows, :] = (sums[:, :HD] / sums[:, HD:]).astype(BF16)
        for dx, dc in OTHERS:
            out_copy(j, partner(s, dx, dc), s).start()
        own_out(j).start()

    loads[0].wait()
    loads[1].wait()

    def prepare_k(i, carry):
        for u in range(SLOTS):
            head = i * SLOTS + u
            kv_src[head, 0] = normed(k_buf, head, k_gain)
            kv_src[head, 1] = v_buf[:, cols(head)]
        return carry

    lax.fori_loop(0, SEQ, prepare_k, 0)
    pl.semaphore_wait(barrier, len(OTHERS) + 2)

    send_kv(0)
    for j in range(SLOTS):
        own_kv(j).start()
    loads[2].wait()

    def prepare_q(i, carry):
        for u in range(SLOTS):
            head = i * SLOTS + u
            q_src[head] = normed(q_buf, head, q_gain)
        return carry

    lax.fori_loop(0, SEQ, prepare_q, 0)
    send_q(0)
    send_kv(1)
    send_kv(2)
    send_q(1)
    send_q(2)
    for j in range(SLOTS):
        own_q(j).start()

    lane = lax.broadcasted_iota(jnp.int32, (8, HD), 1)
    ints[...] = jnp.zeros_like(ints)
    ints[0, :, :SAMPLES] = jnp.broadcast_to(image[...], (8, SAMPLES)) + TXT
    ints[1, :, :SAMPLES] = jnp.broadcast_to(text[...], (8, SAMPLES))
    lengths = ints[0]
    ends = lengths
    step = 1
    while step < SAMPLES:
        ends = ends + jnp.where(lane >= step, pltpu.roll(ends, step, 1), 0)
        step *= 2
    starts = (ends - lengths)[:1]
    ends = ends[:1]
    text_ends = starts + ints[1][:1]
    tokens = groups * GROUP

    def mark(i, carry):
        first = pl.multiple_of(i * 64, 64)
        position = dp * GROUP - HALO + first + lax.broadcasted_iota(jnp.int32, (64, HD), 0)
        position = jnp.where(position < 0, position + tokens, position)
        position = jnp.where(position >= tokens, position - tokens, position)
        inside = (position >= starts) & (position < ends)
        usable = inside & ((position >= starts + TXT) | (position < text_ends))
        mark_k[pl.ds(first, 64), :] = jnp.where(usable, MARK_K, 0.0).astype(BF16)

        @pl.when((i >= HALO // 64) & (i < (HALO + GROUP) // 64))
        def _():
            mark_q[pl.ds(pl.multiple_of(first - HALO, 64), 64), :] = jnp.where(inside, MARK_Q, 0.0).astype(BF16)

        return carry

    lax.fori_loop(0, EXT // 64, mark, 0)

    pass_on(0)
    pass_on(1)
    attend(0)
    pass_on(2)
    attend(1)
    attend(2)

    for j in range(SLOTS):
        for dx, dc in OTHERS:
            out_copy(j, s, partner(s, dx, dc)).wait_recv()
        own_out(j).wait()
    for j in range(SLOTS):
        for index, (dx, dc) in enumerate(OTHERS):
            kv_copy(j, partner(s, dx, dc), s, index).wait_send()
            q_copy(j, partner(s, dx, dc), s, index).wait_send()
            out_copy(j, partner(s, dx, dc), s).wait_send()
        for source in range(2, SEQ):
            left_copy(j, source, 64 if source == 2 else 0).wait_send()
        for source in range(6):
            right_copy(j, source, 64 if source == 5 else ROWS).wait_send()


def solution(mesh):
    groups = mesh.shape["dp"]
    dma = pltpu.SemaphoreType.DMA

    def local(q_in, k_in, v_in, q_gain, k_gain, image_tokens, text_tokens):
        rows, width = q_in.shape
        heads = width // HD
        any_space = pl.BlockSpec(memory_space=pl.ANY)
        vmem = pl.BlockSpec(memory_space=pltpu.VMEM)
        return pl.pallas_call(
            functools.partial(kernel, groups),
            out_shape=jax.ShapeDtypeStruct((rows, width), BF16),
            in_specs=[any_space] * 3 + [vmem] * 4,
            out_specs=any_space,
            scratch_shapes=[
                pltpu.VMEM((rows, width), BF16),
                pltpu.VMEM((rows, width), BF16),
                pltpu.VMEM((rows, width), BF16),
                pltpu.VMEM((heads, 2, rows, HD), BF16),
                pltpu.VMEM((heads, rows, HD), BF16),
                pltpu.VMEM((SLOTS, 2, EXT, HD), BF16),
                pltpu.VMEM((SLOTS, GROUP, HD), BF16),
                pltpu.VMEM((SLOTS, GROUP, HD), BF16),
                pltpu.VMEM((GROUP, HD), BF16),
                pltpu.VMEM((EXT, HD), BF16),
                pltpu.VMEM((2, 8, HD), jnp.int32),
                dma((3,)),
                dma((2, SLOTS)),
                dma((SLOTS, SEQ)),
                dma((SLOTS, SEQ)),
                dma((SLOTS, SEQ)),
                dma((SLOTS, SEQ)),
                dma((SLOTS, SEQ)),
                dma((SLOTS, SEQ)),
                dma((SLOTS, SEQ)),
                dma((SLOTS, SEQ)),
                dma((SLOTS, SEQ)),
                dma((SLOTS, SEQ)),
                dma((SLOTS,)),
            ],
            compiler_params=pltpu.CompilerParams(
                collective_id=0, has_side_effects=True, vmem_limit_bytes=48 * 1024 * 1024
            ),
            cost_estimate=pl.CostEstimate(flops=4_000_000_000, bytes_accessed=4_000_000, transcendentals=5_000_000),
            name="joint_attention",
        )(
            q_in, k_in, v_in,
            q_gain.reshape(1, HD), k_gain.reshape(1, HD),
            image_tokens.reshape(1, SAMPLES), text_tokens.reshape(1, SAMPLES),
        )

    split = P(("dp", "seq"), None)
    return jax.shard_map(
        local,
        mesh=mesh,
        in_specs=(split, split, split, P(), P(), P(), P()),
        out_specs=split,
        check_vma=False,
    )
```

```python
import functools

import jax
import jax.numpy as jnp
from jax import lax
from jax.experimental import pallas as pl
from jax.experimental.pallas import tpu as pltpu
from jax.sharding import PartitionSpec as P

MESH = pl.DeviceIdType.MESH
BF16 = jnp.bfloat16
F32 = jnp.float32

HD = 128
TXT = 128
EPS = 1e-06
SEQ = 8
SLOTS = 3
ROWS = 128
GROUP = SEQ * ROWS
HALO = 704
EXT = GROUP + 2 * HALO
BLOCK = 256
WINDOW = BLOCK + 2 * HALO
SAMPLES = 64
VMEM_BYTES = 53 * 1024 * 1024
NORM_HEADS = 12
K, V = 0, 1

MARK_Q = 64.0
MARK_K = 128.0
SCALE = 1.4426950408889634 / HD**0.5

OTHERS = ((1, 0), (1, 1), (-1, 0), (-1, 1), (2, 0), (2, 1), (0, 1))
ARRIVAL = ((0, 0), (0, 1), (1, 0), (-1, 0), (1, 1), (-1, 1), (2, 0), (2, 1))
NT = (((1,), (1,)), ((), ()))


def partner(s, dx, dc):
    return lax.rem(s // 2 + dx + 4, 4) * 2 + lax.rem(s % 2 + dc, 2)


def kernel(
    groups,
    q_in, k_in, v_in, q_gain, k_gain, image, text,
    out,
    q_buf, k_buf, q_src, k_src, kv_all, q_all, o_buf, mark_q, mark_k, gains, image_buf, text_buf, ints,
    load_sem, own_sem, ready, x_send, z_send, v_recv, kv_recv, q_recv, halo_left, halo_right, out_recv,
):
    dp = lax.axis_index("dp")
    s = lax.axis_index("seq")
    has_after = dp < groups - 1
    has_before = dp > 0
    odd = lax.rem(dp, 2) == 1
    even = jnp.logical_not(odd)
    after = lax.rem(dp + 1, groups)
    before = lax.rem(dp + groups - 1, groups)

    barrier = pltpu.get_barrier_semaphore()
    for dx, dc in OTHERS:
        pl.semaphore_signal(barrier, 1, device_id=(dp, partner(s, dx, dc)), device_id_type=MESH)

    @pl.when(even & has_after)
    def _():
        pl.semaphore_signal(barrier, 1, device_id=(after, s), device_id_type=MESH)

    @pl.when(even & has_before)
    def _():
        pl.semaphore_signal(barrier, 1, device_id=(before, s), device_id_type=MESH)

    small = [
        pltpu.make_async_copy(src, dst, load_sem.at[i])
        for i, (src, dst) in enumerate(
            ((k_gain, gains.at[0]), (q_gain, gains.at[1]), (image, image_buf), (text, text_buf))
        )
    ]
    load_k = pltpu.make_async_copy(k_in, k_buf, load_sem.at[4])
    load_q = pltpu.make_async_copy(q_in, q_buf, load_sem.at[5])
    load_k.start()
    for copy in small:
        copy.start()
    load_q.start()

    def cols(head, count=1):
        return pl.ds(pl.multiple_of(head * HD, HD), count * HD)

    def block(first, count=ROWS):
        return pl.ds(pl.multiple_of(first, 64), count)

    def remote(src, dst, send, recv, dev):
        return pltpu.make_async_remote_copy(
            src_ref=src, dst_ref=dst, send_sem=send, recv_sem=recv, device_id=dev, device_id_type=MESH
        )

    def wait_all(ref, sem):
        pltpu.make_async_copy(ref, ref, sem).wait()

    def source_of(a):
        return k_src if a == K else v_in

    def kv_copy(a, j, to, source):
        recv = v_recv.at[source] if (a, j) == (V, 0) else kv_recv.at[a, j]
        return remote(
            source_of(a).at[:, cols(to * SLOTS + j)], kv_all.at[a, j, block(HALO + source * ROWS), :],
            x_send.at[a], recv, (dp, to),
        )

    def q_copy(j, to, source):
        return remote(
            q_src.at[:, cols(to * SLOTS + j)], q_all.at[j, block(source * ROWS), :],
            x_send.at[2], q_recv.at[j], (dp, to),
        )

    def out_copy(j, to, source):
        return remote(
            o_buf.at[j, block(to * ROWS), :], out.at[:, cols(source * SLOTS + j)],
            x_send.at[3], out_recv.at[j], (dp, to),
        )

    def pass_on(a, j, source, own=False):
        def rows(first, count):
            if own:
                return source_of(a).at[pl.ds(first, count), cols(s * SLOTS + j)]
            return kv_all.at[a, j, block(HALO + source * ROWS + first, count), :]

        def to_after(first, count):
            remote(
                rows(first, count), kv_all.at[a, j, block(source * ROWS + first - (GROUP - HALO), count), :],
                z_send.at[0], halo_left.at[j], (after, s),
            ).start()

        def to_before(count):
            remote(
                rows(0, count), kv_all.at[a, j, block(HALO + GROUP + source * ROWS, count), :],
                z_send.at[1], halo_right.at[j], (before, s),
            ).start()

        @pl.when((source >= 3) & has_after)
        def _():
            to_after(0, ROWS)

        @pl.when((source == 2) & has_after)
        def _():
            to_after(64, ROWS - 64)

        @pl.when((source <= 4) & has_before)
        def _():
            to_before(ROWS)

        @pl.when((source == 5) & has_before)
        def _():
            to_before(64)

    def pass_own():
        for j in range(SLOTS):
            for a in (V, K):
                pass_on(a, j, s, own=True)

    def own_kv(a, j):
        return pltpu.make_async_copy(
            source_of(a).at[:, cols(s * SLOTS + j)], kv_all.at[a, j, block(HALO + s * ROWS), :], own_sem.at[a]
        )

    def own_q(j):
        return pltpu.make_async_copy(
            q_src.at[:, cols(s * SLOTS + j)], q_all.at[j, block(s * ROWS), :], own_sem.at[2]
        )

    def own_out(j):
        return pltpu.make_async_copy(
            o_buf.at[j, block(s * ROWS), :], out.at[:, cols(s * SLOTS + j)], own_sem.at[3]
        )

    def normalize(buf, gain, to):
        def some(i, carry):
            for u in range(NORM_HEADS):
                where = cols(i * NORM_HEADS + u)
                x = buf[:, where].astype(F32)
                square = jnp.sum(x * x, axis=1, keepdims=True) * (1.0 / HD)
                to[:, where] = (x * lax.rsqrt(square + EPS) * gain).astype(BF16)
            return carry

        lax.fori_loop(0, SEQ * SLOTS // NORM_HEADS, some, 0)

    def attend(j):
        wait_all(q_all.at[0, pl.ds(0, len(OTHERS) * ROWS), :], q_recv.at[j])

        @pl.when(has_before)
        def _():
            wait_all(kv_all.at[K, 0, pl.ds(0, 2 * HALO), :], halo_left.at[j])

        @pl.when(has_after)
        def _():
            wait_all(kv_all.at[K, 0, pl.ds(0, 2 * HALO), :], halo_right.at[j])

        for i in range(GROUP // BLOCK):
            rows, window = pl.ds(i * BLOCK, BLOCK), pl.ds(i * BLOCK, WINDOW)
            q = jnp.concatenate([q_all[j, rows, :], mark_q[rows, :]], axis=1)
            k = jnp.concatenate([kv_all[K, j, window, :], mark_k[window, :]], axis=1)
            v = kv_all[V, j, window, :]
            scores = lax.dot_general(q, k, NT, preferred_element_type=F32)
            top = jnp.max(scores, axis=1, keepdims=True)
            weights = jnp.exp2((scores - top) * SCALE).astype(BF16)
            sums = jnp.dot(weights, jnp.concatenate([v, jnp.ones_like(v)], axis=1), preferred_element_type=F32)
            o_buf[j, rows, :] = (sums[:, :HD] / sums[:, HD:]).astype(BF16)
        for dx, dc in OTHERS:
            out_copy(j, partner(s, dx, dc), s).start()
        own_out(j).start()

    load_k.wait()
    for copy in small:
        copy.wait()
    normalize(k_buf, gains[0], k_src)

    @pl.when(even)
    def _():
        pl.semaphore_wait(barrier, len(OTHERS))

    @pl.when(odd & has_after)
    def _():
        pl.semaphore_wait(barrier, len(OTHERS) + 2)

    @pl.when(odd & jnp.logical_not(has_after))
    def _():
        pl.semaphore_wait(barrier, len(OTHERS) + 1)

    def send_kv(a, j):
        for dx, dc in OTHERS:
            kv_copy(a, j, partner(s, dx, dc), s).start()

    send_kv(V, 0)

    @pl.when(odd)
    def _():
        pl.semaphore_signal(ready, 1, device_id=(before, s), device_id_type=MESH)

    @pl.when(odd & has_after)
    def _():
        pl.semaphore_signal(ready, 1, device_id=(after, s), device_id_type=MESH)

    send_kv(K, 0)

    @pl.when(odd)
    def _():
        pass_own()

    for j in range(1, SLOTS):
        send_kv(V, j)
        send_kv(K, j)
    for j in range(SLOTS):
        own_kv(K, j).start()
        own_kv(V, j).start()
    load_q.wait()
    normalize(q_buf, gains[1], q_src)
    for j in range(SLOTS):
        for dx, dc in OTHERS:
            q_copy(j, partner(s, dx, dc), s).start()
        own_q(j).start()

    @pl.when(even & has_after & has_before)
    def _():
        pl.semaphore_wait(ready, 2)

    @pl.when(even & jnp.logical_not(has_after & has_before))
    def _():
        pl.semaphore_wait(ready, 1)

    @pl.when(even)
    def _():
        pass_own()

    for j in range(SLOTS):
        for a in (V, K):
            if (a, j) != (V, 0):
                wait_all(kv_all.at[a, 0, pl.ds(0, len(OTHERS) * ROWS), :], kv_recv.at[a, j])
            for dx, dc in ARRIVAL[1:]:
                source = partner(s, dx, dc)
                if (a, j) == (V, 0):
                    kv_copy(V, 0, s, source).wait_recv()
                pass_on(a, j, source)

    @pl.when(jnp.logical_not(has_before))
    def _():
        kv_all[:, :, pl.ds(0, HALO), :] = jnp.zeros((2, SLOTS, HALO, HD), BF16)

    @pl.when(jnp.logical_not(has_after))
    def _():
        kv_all[:, :, pl.ds(HALO + GROUP, HALO), :] = jnp.zeros((2, SLOTS, HALO, HD), BF16)

    lane = lax.broadcasted_iota(jnp.int32, (8, HD), 1)
    ints[...] = jnp.zeros_like(ints)
    ints[0, :, :SAMPLES] = jnp.broadcast_to(image_buf[...] + TXT, (8, SAMPLES))
    ints[1, :, :SAMPLES] = jnp.broadcast_to(text_buf[...], (8, SAMPLES))
    lengths = ints[0]
    ends = lengths
    step = 1
    while step < SAMPLES:
        ends = ends + jnp.where(lane >= step, pltpu.roll(ends, step, 1), 0)
        step *= 2
    starts = (ends - lengths)[:1]
    ends = ends[:1]
    text_ends = starts + ints[1][:1]

    def mark(i, carry):
        first = pl.multiple_of(i * 64, 64)
        position = dp * GROUP - HALO + first + lax.broadcasted_iota(jnp.int32, (64, HD), 0)
        inside = (position >= starts) & (position < ends)
        usable = inside & ((position >= starts + TXT) | (position < text_ends))
        mark_k[pl.ds(first, 64), :] = jnp.where(usable, MARK_K, 0.0).astype(BF16)

        @pl.when((i >= HALO // 64) & (i < (HALO + GROUP) // 64))
        def _():
            mark_q[pl.ds(pl.multiple_of(first - HALO, 64), 64), :] = jnp.where(inside, MARK_Q, 0.0).astype(BF16)

        return carry

    lax.fori_loop(0, EXT // 64, mark, 0)

    own_rows = block(s * ROWS)
    own_ext = block(HALO + s * ROWS)
    wait_all(kv_all.at[K, :, own_ext, :], own_sem.at[0])
    wait_all(kv_all.at[V, :, own_ext, :], own_sem.at[1])
    wait_all(q_all.at[:, own_rows, :], own_sem.at[2])
    for j in range(SLOTS):
        attend(j)

    sent = k_src.at[:, pl.ds(0, len(OTHERS) * SLOTS * HD)]
    for i in range(3):
        wait_all(sent, x_send.at[i])

    @pl.when(has_after)
    def _():
        wait_all(kv_all.at[:, :, pl.ds(0, HALO), :], z_send.at[0])

    @pl.when(has_before)
    def _():
        wait_all(kv_all.at[:, :, pl.ds(0, HALO), :], z_send.at[1])

    wait_all(o_buf.at[:, own_rows, :], own_sem.at[3])
    for j in range(SLOTS):
        wait_all(out.at[:, pl.ds(0, len(OTHERS) * HD)], out_recv.at[j])
    wait_all(sent, x_send.at[3])


def solution(mesh):
    groups = mesh.shape["dp"]
    dma = pltpu.SemaphoreType.DMA

    def local(q_in, k_in, v_in, q_gain, k_gain, image_tokens, text_tokens):
        rows, width = q_in.shape
        return pl.pallas_call(
            functools.partial(kernel, groups),
            out_shape=jax.ShapeDtypeStruct((rows, width), BF16),
            in_specs=[pl.BlockSpec(memory_space=pltpu.HBM)] * 7,
            out_specs=pl.BlockSpec(memory_space=pl.ANY),
            scratch_shapes=[
                pltpu.VMEM((rows, width), BF16),
                pltpu.VMEM((rows, width), BF16),
                pltpu.VMEM((rows, width), BF16),
                pltpu.VMEM((rows, width), BF16),
                pltpu.VMEM((2, SLOTS, EXT, HD), BF16),
                pltpu.VMEM((SLOTS, GROUP, HD), BF16),
                pltpu.VMEM((SLOTS, GROUP, HD), BF16),
                pltpu.VMEM((GROUP, HD), BF16),
                pltpu.VMEM((EXT, HD), BF16),
                pltpu.VMEM((2, 1, HD), F32),
                pltpu.VMEM((1, SAMPLES), jnp.int32),
                pltpu.VMEM((1, SAMPLES), jnp.int32),
                pltpu.VMEM((2, 8, HD), jnp.int32),
                dma((6,)),
                dma((4,)),
                pltpu.SemaphoreType.REGULAR,
                dma((4,)),
                dma((2,)),
                dma((SEQ,)),
                dma((2, SLOTS)),
                dma((SLOTS,)),
                dma((SLOTS,)),
                dma((SLOTS,)),
                dma((SLOTS,)),
            ],
            compiler_params=pltpu.CompilerParams(
                collective_id=0, has_side_effects=True, vmem_limit_bytes=VMEM_BYTES
            ),
            cost_estimate=pl.CostEstimate(flops=4_000_000_000, bytes_accessed=4_000_000, transcendentals=5_000_000),
            name="joint_attention",
        )(
            q_in, k_in, v_in,
            q_gain.reshape(1, HD), k_gain.reshape(1, HD),
            image_tokens.reshape(1, SAMPLES), text_tokens.reshape(1, SAMPLES),
        )

    split = P(("dp", "seq"), None)
    return jax.shard_map(
        local,
        mesh=mesh,
        in_specs=(split, split, split, P(), P(), P(), P()),
        out_specs=split,
        check_vma=False,
    )
```

```python
import functools

import jax
import jax.numpy as jnp
from jax import lax
from jax.experimental import pallas as pl
from jax.experimental.pallas import tpu as pltpu
from jax.sharding import PartitionSpec as P

MESH = pl.DeviceIdType.MESH
BF16 = jnp.bfloat16
F32 = jnp.float32

HD = 128
TXT = 128
EPS = 1e-06
SEQ = 8
SLOTS = 3
ROWS = 128
GROUP = SEQ * ROWS
HALO = 704
EXT = GROUP + 2 * HALO
BLOCK = 256
WINDOW = BLOCK + 2 * HALO
SAMPLES = 64
VMEM_BYTES = 53 * 1024 * 1024
NORM_HEADS = 12
K, V, Q = 0, 1, 2
NEAR, FAR = 0, 1
ORDER = ((V, 0), (K, 0), (V, 1), (K, 1), (V, 2), (K, 2), (Q, 0), (Q, 1), (Q, 2))
AHEAD = 4

MARK_Q = 64.0
MARK_K = 128.0
SCALE = 1.4426950408889634 / HD**0.5

OTHERS = ((1, 0), (-1, 0), (2, 0), (1, 1), (-1, 1), (2, 1), (0, 1))
ARRIVAL = ((0, 1), (1, 0), (-1, 0), (1, 1), (-1, 1), (2, 0), (2, 1))
NT = (((1,), (1,)), ((), ()))


def partner(s, dx, dc):
    return lax.rem(s // 2 + dx + 4, 4) * 2 + lax.rem(s % 2 + dc, 2)


def kernel(
    groups,
    q_in, k_in, v_in, q_gain, k_gain, image, text,
    out,
    q_buf, k_buf, q_src, k_src, kv_all, q_all, o_buf, mark_q, mark_k, gains, image_buf, text_buf, ints,
    load_sem, own_sem, ready, x_send, z_send, v_recv, kv_recv, q_recv, halo_left, halo_right, out_recv,
):
    dp = lax.axis_index("dp")
    s = lax.axis_index("seq")
    has_after = dp < groups - 1
    has_before = dp > 0
    odd = lax.rem(dp, 2) == 1
    even = jnp.logical_not(odd)
    after = lax.rem(dp + 1, groups)
    before = lax.rem(dp + groups - 1, groups)

    barrier = pltpu.get_barrier_semaphore()
    for dx, dc in OTHERS:
        pl.semaphore_signal(barrier, 1, device_id=(dp, partner(s, dx, dc)), device_id_type=MESH)

    @pl.when(even & has_after)
    def _():
        pl.semaphore_signal(barrier, 1, device_id=(after, s), device_id_type=MESH)

    @pl.when(even & has_before)
    def _():
        pl.semaphore_signal(barrier, 1, device_id=(before, s), device_id_type=MESH)

    small = [
        pltpu.make_async_copy(src, dst, load_sem.at[i])
        for i, (src, dst) in enumerate(
            ((k_gain, gains.at[0]), (q_gain, gains.at[1]), (image, image_buf), (text, text_buf))
        )
    ]
    load_k = pltpu.make_async_copy(k_in, k_buf, load_sem.at[4])
    load_q = pltpu.make_async_copy(q_in, q_buf, load_sem.at[5])
    load_k.start()
    for copy in small:
        copy.start()
    load_q.start()

    def cols(head, count=1):
        return pl.ds(pl.multiple_of(head * HD, HD), count * HD)

    def block(first, count=ROWS):
        return pl.ds(pl.multiple_of(first, 64), count)

    def remote(src, dst, send, recv, dev):
        return pltpu.make_async_remote_copy(
            src_ref=src, dst_ref=dst, send_sem=send, recv_sem=recv, device_id=dev, device_id_type=MESH
        )

    def wait_all(ref, sem):
        pltpu.make_async_copy(ref, ref, sem).wait()

    def source_of(a):
        return k_src if a == K else v_in

    def kv_copy(a, j, to, source):
        recv = v_recv.at[source] if (a, j) == (V, 0) else kv_recv.at[a, j]
        return remote(
            source_of(a).at[:, cols(to * SLOTS + j)], kv_all.at[a, j, block(HALO + source * ROWS), :],
            x_send.at[a], recv, (dp, to),
        )

    def q_copy(j, to, source):
        return remote(
            q_src.at[:, cols(to * SLOTS + j)], q_all.at[j, block(source * ROWS), :],
            x_send.at[2], q_recv.at[j], (dp, to),
        )

    def out_copy(j, to, source):
        return remote(
            o_buf.at[j, block(to * ROWS), :], out.at[:, cols(source * SLOTS + j)],
            x_send.at[3], out_recv.at[j], (dp, to),
        )

    def pass_on(a, j, source, own=False):
        def rows(first, count):
            if own:
                return source_of(a).at[pl.ds(first, count), cols(s * SLOTS + j)]
            return kv_all.at[a, j, block(HALO + source * ROWS + first, count), :]

        def to_after(first, count, sem):
            remote(
                rows(first, count), kv_all.at[a, j, block(source * ROWS + first - (GROUP - HALO), count), :],
                z_send.at[0], sem, (after, s),
            ).start()

        def to_before(count, sem):
            remote(
                rows(0, count), kv_all.at[a, j, block(HALO + GROUP + source * ROWS, count), :],
                z_send.at[1], sem, (before, s),
            ).start()

        @pl.when((source >= 6) & has_after)
        def _():
            to_after(0, ROWS, halo_left.at[NEAR, j])

        @pl.when((source >= 3) & (source < 6) & has_after)
        def _():
            to_after(0, ROWS, halo_left.at[FAR, j])

        @pl.when((source == 2) & has_after)
        def _():
            to_after(64, ROWS - 64, halo_left.at[FAR, j])

        @pl.when((source < 2) & has_before)
        def _():
            to_before(ROWS, halo_right.at[NEAR, j])

        @pl.when((source >= 2) & (source <= 4) & has_before)
        def _():
            to_before(ROWS, halo_right.at[FAR, j])

        @pl.when((source == 5) & has_before)
        def _():
            to_before(64, halo_right.at[FAR, j])

    def pass_own(a):
        for j in range(SLOTS):
            pass_on(a, j, s, own=True)

    def own_kv(a, j):
        return pltpu.make_async_copy(
            source_of(a).at[:, cols(s * SLOTS + j)], kv_all.at[a, j, block(HALO + s * ROWS), :], own_sem.at[a]
        )

    def own_q(j):
        return pltpu.make_async_copy(
            q_src.at[:, cols(s * SLOTS + j)], q_all.at[j, block(s * ROWS), :], own_sem.at[2]
        )

    def own_out(j):
        return pltpu.make_async_copy(
            o_buf.at[j, block(s * ROWS), :], out.at[:, cols(s * SLOTS + j)], own_sem.at[3]
        )

    def normalize(buf, gain, to):
        def some(i, carry):
            for u in range(NORM_HEADS):
                where = cols(i * NORM_HEADS + u)
                x = buf[:, where].astype(F32)
                square = jnp.sum(x * x, axis=1, keepdims=True) * (1.0 / HD)
                to[:, where] = (x * lax.rsqrt(square + EPS) * gain).astype(BF16)
            return carry

        lax.fori_loop(0, SEQ * SLOTS // NORM_HEADS, some, 0)

    def wait_halo(sems, part, j, present):
        count = 2 * (2 * ROWS if part == NEAR else HALO - 2 * ROWS)

        @pl.when(present)
        def _():
            wait_all(kv_all.at[K, 0, pl.ds(0, count), :], sems.at[part, j])

    def attend(j, first, blocks):
        for i in range(blocks):
            start = first + i * BLOCK
            if not isinstance(start, int):
                start = pl.multiple_of(start, BLOCK)
            rows, window = pl.ds(start, BLOCK), pl.ds(start, WINDOW)
            q = jnp.concatenate([q_all[j, rows, :], mark_q[rows, :]], axis=1)
            k = jnp.concatenate([kv_all[K, j, window, :], mark_k[window, :]], axis=1)
            v = kv_all[V, j, window, :]
            scores = lax.dot_general(q, k, NT, preferred_element_type=F32)
            top = jnp.max(scores, axis=1, keepdims=True)
            weights = jnp.exp2((scores - top) * SCALE).astype(BF16)
            sums = jnp.dot(weights, jnp.concatenate([v, jnp.ones_like(v)], axis=1), preferred_element_type=F32)
            o_buf[j, rows, :] = (sums[:, :HD] / sums[:, HD:]).astype(BF16)

    def attend_whole(j):
        wait_all(q_all.at[0, pl.ds(0, len(OTHERS) * ROWS), :], q_recv.at[j])
        for part in (NEAR, FAR):
            wait_halo(halo_left, part, j, has_before)
            wait_halo(halo_right, part, j, has_after)
        attend(j, 0, GROUP // BLOCK)
        for dx, dc in OTHERS:
            out_copy(j, partner(s, dx, dc), s).start()
        own_out(j).start()

    def attend_halves(j):
        wait_all(q_all.at[0, pl.ds(0, len(OTHERS) * ROWS), :], q_recv.at[j])
        wait_halo(halo_left, NEAR, j, has_before)
        wait_halo(halo_right, NEAR, j, has_after)
        place = lax.rem(dp, 8)
        left_late = (place == 0) | (place == 7) | (s < 4)
        for upper in (left_late, jnp.logical_not(left_late)):
            wait_halo(halo_right, FAR, j, upper & has_after)
            wait_halo(halo_left, FAR, j, jnp.logical_not(upper) & has_before)
            half = jnp.where(upper, 1, 0)
            attend(j, half * (GROUP // 2), GROUP // 2 // BLOCK)
            for i in range(SEQ // 2):
                to = half * (SEQ // 2) + i

                @pl.when(to != s)
                def _():
                    out_copy(j, to, s).start()

                @pl.when(to == s)
                def _():
                    own_out(j).start()

    @pl.when(even)
    def _():
        pl.semaphore_wait(barrier, len(OTHERS))

    @pl.when(odd & has_after)
    def _():
        pl.semaphore_wait(barrier, len(OTHERS) + 2)

    @pl.when(odd & jnp.logical_not(has_after))
    def _():
        pl.semaphore_wait(barrier, len(OTHERS) + 1)

    def send(a, j):
        for dx, dc in OTHERS:
            to = partner(s, dx, dc)
            (q_copy(j, to, s) if a == Q else kv_copy(a, j, to, s)).start()

    send(V, 0)

    @pl.when(odd)
    def _():
        pl.semaphore_signal(ready, 1, device_id=(before, s), device_id_type=MESH)

    @pl.when(odd & has_after)
    def _():
        pl.semaphore_signal(ready, 1, device_id=(after, s), device_id_type=MESH)

    @pl.when(odd)
    def _():
        pass_own(V)

    load_k.wait()
    for copy in small:
        copy.wait()
    normalize(k_buf, gains[0], k_src)
    send(K, 0)

    @pl.when(odd)
    def _():
        pass_own(K)

    for a, j in ORDER[2:AHEAD]:
        send(a, j)
    for j in range(SLOTS):
        own_kv(K, j).start()
        own_kv(V, j).start()
    load_q.wait()
    normalize(q_buf, gains[1], q_src)
    for j in range(SLOTS):
        own_q(j).start()

    @pl.when(even & has_after & has_before)
    def _():
        pl.semaphore_wait(ready, 2)

    @pl.when(even & jnp.logical_not(has_after & has_before))
    def _():
        pl.semaphore_wait(ready, 1)

    @pl.when(even)
    def _():
        pass_own(V)
        pass_own(K)

    for at, (a, j) in enumerate(ORDER[:6]):
        if at > 0:
            wait_all(kv_all.at[a, 0, pl.ds(0, len(OTHERS) * ROWS), :], kv_recv.at[a, j])
        for dx, dc in ARRIVAL:
            source = partner(s, dx, dc)
            if at == 0:
                kv_copy(a, j, s, source).wait_recv()
            pass_on(a, j, source)
        if at + AHEAD < len(ORDER):
            send(*ORDER[at + AHEAD])

    @pl.when(jnp.logical_not(has_before))
    def _():
        kv_all[:, :, pl.ds(0, HALO), :] = jnp.zeros((2, SLOTS, HALO, HD), BF16)

    @pl.when(jnp.logical_not(has_after))
    def _():
        kv_all[:, :, pl.ds(HALO + GROUP, HALO), :] = jnp.zeros((2, SLOTS, HALO, HD), BF16)

    lane = lax.broadcasted_iota(jnp.int32, (8, HD), 1)
    ints[...] = jnp.zeros_like(ints)
    ints[0, :, :SAMPLES] = jnp.broadcast_to(image_buf[...] + TXT, (8, SAMPLES))
    ints[1, :, :SAMPLES] = jnp.broadcast_to(text_buf[...], (8, SAMPLES))
    lengths = ints[0]
    ends = lengths
    step = 1
    while step < SAMPLES:
        ends = ends + jnp.where(lane >= step, pltpu.roll(ends, step, 1), 0)
        step *= 2
    starts = (ends - lengths)[:1]
    ends = ends[:1]
    text_ends = starts + ints[1][:1]

    def mark(i, carry):
        first = pl.multiple_of(i * 64, 64)
        position = dp * GROUP - HALO + first + lax.broadcasted_iota(jnp.int32, (64, HD), 0)
        inside = (position >= starts) & (position < ends)
        usable = inside & ((position >= starts + TXT) | (position < text_ends))
        mark_k[pl.ds(first, 64), :] = jnp.where(usable, MARK_K, 0.0).astype(BF16)

        @pl.when((i >= HALO // 64) & (i < (HALO + GROUP) // 64))
        def _():
            mark_q[pl.ds(pl.multiple_of(first - HALO, 64), 64), :] = jnp.where(inside, MARK_Q, 0.0).astype(BF16)

        return carry

    lax.fori_loop(0, EXT // 64, mark, 0)

    own_rows = block(s * ROWS)
    own_ext = block(HALO + s * ROWS)
    wait_all(kv_all.at[K, :, own_ext, :], own_sem.at[0])
    wait_all(kv_all.at[V, :, own_ext, :], own_sem.at[1])
    wait_all(q_all.at[:, own_rows, :], own_sem.at[2])
    for j in range(SLOTS - 1):
        attend_whole(j)
    attend_halves(SLOTS - 1)

    sent = k_src.at[:, pl.ds(0, len(OTHERS) * SLOTS * HD)]
    for i in range(3):
        wait_all(sent, x_send.at[i])

    @pl.when(has_after)
    def _():
        wait_all(kv_all.at[:, :, pl.ds(0, HALO), :], z_send.at[0])

    @pl.when(has_before)
    def _():
        wait_all(kv_all.at[:, :, pl.ds(0, HALO), :], z_send.at[1])

    wait_all(o_buf.at[:, own_rows, :], own_sem.at[3])
    for j in range(SLOTS):
        wait_all(out.at[:, pl.ds(0, len(OTHERS) * HD)], out_recv.at[j])
    wait_all(sent, x_send.at[3])


def solution(mesh):
    groups = mesh.shape["dp"]
    dma = pltpu.SemaphoreType.DMA

    def local(q_in, k_in, v_in, q_gain, k_gain, image_tokens, text_tokens):
        rows, width = q_in.shape
        return pl.pallas_call(
            functools.partial(kernel, groups),
            out_shape=jax.ShapeDtypeStruct((rows, width), BF16),
            in_specs=[pl.BlockSpec(memory_space=pltpu.HBM)] * 7,
            out_specs=pl.BlockSpec(memory_space=pl.ANY),
            scratch_shapes=[
                pltpu.VMEM((rows, width), BF16),
                pltpu.VMEM((rows, width), BF16),
                pltpu.VMEM((rows, width), BF16),
                pltpu.VMEM((rows, width), BF16),
                pltpu.VMEM((2, SLOTS, EXT, HD), BF16),
                pltpu.VMEM((SLOTS, GROUP, HD), BF16),
                pltpu.VMEM((SLOTS, GROUP, HD), BF16),
                pltpu.VMEM((GROUP, HD), BF16),
                pltpu.VMEM((EXT, HD), BF16),
                pltpu.VMEM((2, 1, HD), F32),
                pltpu.VMEM((1, SAMPLES), jnp.int32),
                pltpu.VMEM((1, SAMPLES), jnp.int32),
                pltpu.VMEM((2, 8, HD), jnp.int32),
                dma((6,)),
                dma((4,)),
                pltpu.SemaphoreType.REGULAR,
                dma((4,)),
                dma((2,)),
                dma((SEQ,)),
                dma((2, SLOTS)),
                dma((SLOTS,)),
                dma((2, SLOTS)),
                dma((2, SLOTS)),
                dma((SLOTS,)),
            ],
            compiler_params=pltpu.CompilerParams(
                collective_id=0, has_side_effects=True, vmem_limit_bytes=VMEM_BYTES
            ),
            cost_estimate=pl.CostEstimate(flops=4_000_000_000, bytes_accessed=4_000_000, transcendentals=5_000_000),
            name="joint_attention",
        )(
            q_in, k_in, v_in,
            q_gain.reshape(1, HD), k_gain.reshape(1, HD),
            image_tokens.reshape(1, SAMPLES), text_tokens.reshape(1, SAMPLES),
        )

    split = P(("dp", "seq"), None)
    return jax.shard_map(
        local,
        mesh=mesh,
        in_specs=(split, split, split, P(), P(), P(), P()),
        out_specs=split,
        check_vma=False,
    )
```

```python
import functools

import jax
import jax.numpy as jnp
from jax import lax
from jax.experimental import pallas as pl
from jax.experimental.pallas import tpu as pltpu
from jax.sharding import PartitionSpec as P

MESH = pl.DeviceIdType.MESH
BF16 = jnp.bfloat16
F32 = jnp.float32

HD = 128
TXT = 128
EPS = 1e-06
SEQ = 8
SLOTS = 3
ROWS = 128
GROUP = SEQ * ROWS
HALO = 704
EXT = GROUP + 2 * HALO
BLOCK = 256
WINDOW = BLOCK + 2 * HALO
SAMPLES = 64
VMEM_BYTES = 48 * 1024 * 1024
NORM_HEADS = 12
K, V, Q = 0, 1, 2
PARTS = 3
ORDER = ((V, 0), (K, 0), (V, 1), (K, 1), (V, 2), (K, 2), (Q, 0), (Q, 1), (Q, 2))
AHEAD = 4

MARK_Q = 64.0
MARK_K = 128.0
SCALE = 1.4426950408889634 / HD**0.5

OTHERS = ((1, 0), (-1, 0), (2, 0), (1, 1), (-1, 1), (2, 1), (0, 1))
ARRIVAL = ((0, 1), (1, 0), (-1, 0), (1, 1), (-1, 1), (2, 0), (2, 1))
NT = (((1,), (1,)), ((), ()))


def partner(s, dx, dc):
    return lax.rem(s // 2 + dx + 4, 4) * 2 + lax.rem(s % 2 + dc, 2)


def kernel(
    groups,
    q_in, k_in, v_in, q_gain, k_gain, image, text,
    out,
    q_buf, k_buf, q_src, k_src, kv_all, q_all, o_buf, mark_q, mark_k, gains, image_buf, text_buf, ints,
    load_sem, own_sem, ready, x_send, z_send, v_recv, kv_recv, q_recv, halo_left, halo_right, out_recv,
):
    dp = lax.axis_index("dp")
    s = lax.axis_index("seq")
    has_after = dp < groups - 1
    has_before = dp > 0
    odd = lax.rem(dp, 2) == 1
    even = jnp.logical_not(odd)
    after = lax.rem(dp + 1, groups)
    before = lax.rem(dp + groups - 1, groups)

    barrier = pltpu.get_barrier_semaphore()
    for dx, dc in OTHERS:
        pl.semaphore_signal(barrier, 1, device_id=(dp, partner(s, dx, dc)), device_id_type=MESH)

    @pl.when(even & has_after)
    def _():
        pl.semaphore_signal(barrier, 1, device_id=(after, s), device_id_type=MESH)

    @pl.when(even & has_before)
    def _():
        pl.semaphore_signal(barrier, 1, device_id=(before, s), device_id_type=MESH)

    small = [
        pltpu.make_async_copy(src, dst, load_sem.at[i])
        for i, (src, dst) in enumerate(
            ((k_gain, gains.at[0]), (q_gain, gains.at[1]), (image, image_buf), (text, text_buf))
        )
    ]
    load_k = pltpu.make_async_copy(k_in, k_buf, load_sem.at[4])
    load_q = pltpu.make_async_copy(q_in, q_buf, load_sem.at[5])
    load_k.start()
    for copy in small:
        copy.start()
    load_q.start()

    def cols(head, count=1):
        return pl.ds(pl.multiple_of(head * HD, HD), count * HD)

    def block(first, count=ROWS):
        return pl.ds(pl.multiple_of(first, 64), count)

    def remote(src, dst, send, recv, dev):
        return pltpu.make_async_remote_copy(
            src_ref=src, dst_ref=dst, send_sem=send, recv_sem=recv, device_id=dev, device_id_type=MESH
        )

    def wait_all(ref, sem):
        pltpu.make_async_copy(ref, ref, sem).wait()

    def source_of(a):
        return k_src if a == K else v_in

    def kv_copy(a, j, to, source):
        recv = v_recv.at[source] if (a, j) == (V, 0) else kv_recv.at[a, j]
        return remote(
            source_of(a).at[:, cols(to * SLOTS + j)], kv_all.at[a, j, block(HALO + source * ROWS), :],
            x_send.at[a], recv, (dp, to),
        )

    def q_copy(j, to, source):
        return remote(
            q_src.at[:, cols(to * SLOTS + j)], q_all.at[j, block(source * ROWS), :],
            x_send.at[2], q_recv.at[j], (dp, to),
        )

    def out_copy(j, to, source):
        return remote(
            o_buf.at[j, block(to * ROWS), :], out.at[:, cols(source * SLOTS + j)],
            x_send.at[3], out_recv.at[j], (dp, to),
        )

    def halo_rows(a, j, source, first, count, own):
        if own:
            return source_of(a).at[pl.ds(first, count), cols(s * SLOTS + j)]
        return kv_all.at[a, j, block(HALO + source * ROWS + first, count), :]

    def pass_after(a, j, source, own=False):
        def start(first):
            remote(
                halo_rows(a, j, source, first, ROWS - first, own),
                kv_all.at[a, j, block(source * ROWS + first - (GROUP - HALO), ROWS - first), :],
                z_send.at[0], halo_left.at[(SEQ - 1 - source) // 2, j], (after, s),
            ).start()

        @pl.when((source >= 3) & has_after)
        def _():
            start(0)

        @pl.when((source == 2) & has_after)
        def _():
            start(64)

    def pass_before(a, j, source, own=False):
        def start(count):
            remote(
                halo_rows(a, j, source, 0, count, own),
                kv_all.at[a, j, block(HALO + GROUP + source * ROWS, count), :],
                z_send.at[1], halo_right.at[source // 2, j], (before, s),
            ).start()

        @pl.when((source <= 4) & has_before)
        def _():
            start(ROWS)

        @pl.when((source == 5) & has_before)
        def _():
            start(64)

    def pass_own(a):
        for j in range(SLOTS):
            pass_after(a, j, s, own=True)
            pass_before(a, j, s, own=True)

    def pass_part(a, j, part):
        for source in (2 * part, 2 * part + 1):
            mirror = SEQ - 1 - source

            @pl.when(mirror != s)
            def _():
                pass_after(a, j, mirror)

            @pl.when(source != s)
            def _():
                pass_before(a, j, source)

    def own_kv(a, j):
        return pltpu.make_async_copy(
            source_of(a).at[:, cols(s * SLOTS + j)], kv_all.at[a, j, block(HALO + s * ROWS), :], own_sem.at[a]
        )

    def own_q(j):
        return pltpu.make_async_copy(
            q_src.at[:, cols(s * SLOTS + j)], q_all.at[j, block(s * ROWS), :], own_sem.at[2]
        )

    def own_out(j):
        return pltpu.make_async_copy(
            o_buf.at[j, block(s * ROWS), :], out.at[:, cols(s * SLOTS + j)], own_sem.at[3]
        )

    def normalize(buf, gain, to):
        def some(i, carry):
            for u in range(NORM_HEADS):
                where = cols(i * NORM_HEADS + u)
                x = buf[:, where].astype(F32)
                square = jnp.sum(x * x, axis=1, keepdims=True) * (1.0 / HD)
                to[:, where] = (x * lax.rsqrt(square + EPS) * gain).astype(BF16)
            return carry

        lax.fori_loop(0, SEQ * SLOTS // NORM_HEADS, some, 0)

    def wait_halo(sems, part, j, present):
        count = 2 * min(2 * ROWS, HALO - part * 2 * ROWS)

        @pl.when(present)
        def _():
            wait_all(kv_all.at[K, 0, pl.ds(0, count), :], sems.at[part, j])

    def attend(j, first, blocks):
        for i in range(blocks):
            start = first + i * BLOCK
            if not isinstance(start, int):
                start = pl.multiple_of(start, BLOCK)
            rows, window = pl.ds(start, BLOCK), pl.ds(start, WINDOW)
            q = jnp.concatenate([q_all[j, rows, :], mark_q[rows, :]], axis=1)
            k = jnp.concatenate([kv_all[K, j, window, :], mark_k[window, :]], axis=1)
            v = kv_all[V, j, window, :]
            scores = lax.dot_general(q, k, NT, preferred_element_type=F32)
            top = jnp.max(scores, axis=1, keepdims=True)
            weights = jnp.exp2((scores - top) * SCALE).astype(BF16)
            sums = jnp.dot(weights, jnp.concatenate([v, jnp.ones_like(v)], axis=1), preferred_element_type=F32)
            o_buf[j, rows, :] = (sums[:, :HD] / sums[:, HD:]).astype(BF16)

    def attend_whole(j):
        wait_all(q_all.at[0, pl.ds(0, len(OTHERS) * ROWS), :], q_recv.at[j])
        for part in range(PARTS):
            wait_halo(halo_left, part, j, has_before)
            wait_halo(halo_right, part, j, has_after)
        attend(j, 0, GROUP // BLOCK)
        for dx, dc in OTHERS:
            out_copy(j, partner(s, dx, dc), s).start()
        own_out(j).start()

    def attend_steps(j):
        wait_all(q_all.at[0, pl.ds(0, len(OTHERS) * ROWS), :], q_recv.at[j])
        wait_halo(halo_left, 0, j, has_before)
        wait_halo(halo_right, 0, j, has_after)
        left_late = s < SEQ // 2
        right_late = jnp.logical_not(left_late)
        for part in range(1, PARTS):
            wait_halo(halo_right, part, j, left_late & has_after)
            wait_halo(halo_left, part, j, right_late & has_before)
        for part, (upward, downward, blocks) in enumerate(((2, 0, 2), (1, 2, 1), (0, 3, 1))):
            if part > 0:
                wait_halo(halo_left, part, j, left_late & has_before)
                wait_halo(halo_right, part, j, right_late & has_after)
            first = jnp.where(left_late, upward, downward)
            attend(j, first * BLOCK, blocks)
            for i in range(blocks * BLOCK // ROWS):
                to = first * (BLOCK // ROWS) + i

                @pl.when(to != s)
                def _():
                    out_copy(j, to, s).start()

                @pl.when(to == s)
                def _():
                    own_out(j).start()

    @pl.when(even)
    def _():
        pl.semaphore_wait(barrier, len(OTHERS))

    @pl.when(odd & has_after)
    def _():
        pl.semaphore_wait(barrier, len(OTHERS) + 2)

    @pl.when(odd & jnp.logical_not(has_after))
    def _():
        pl.semaphore_wait(barrier, len(OTHERS) + 1)

    def send(a, j):
        for dx, dc in OTHERS:
            to = partner(s, dx, dc)
            (q_copy(j, to, s) if a == Q else kv_copy(a, j, to, s)).start()

    send(V, 0)

    @pl.when(odd)
    def _():
        pl.semaphore_signal(ready, 1, device_id=(before, s), device_id_type=MESH)

    @pl.when(odd & has_after)
    def _():
        pl.semaphore_signal(ready, 1, device_id=(after, s), device_id_type=MESH)

    @pl.when(odd)
    def _():
        pass_own(V)

    load_k.wait()
    for copy in small:
        copy.wait()
    normalize(k_buf, gains[0], k_src)
    send(K, 0)

    @pl.when(odd)
    def _():
        pass_own(K)

    for a, j in ORDER[2:AHEAD]:
        send(a, j)
    for j in range(SLOTS):
        own_kv(K, j).start()
        own_kv(V, j).start()
    load_q.wait()
    normalize(q_buf, gains[1], q_src)
    for j in range(SLOTS):
        own_q(j).start()

    @pl.when(even & has_after & has_before)
    def _():
        pl.semaphore_wait(ready, 2)

    @pl.when(even & jnp.logical_not(has_after & has_before))
    def _():
        pl.semaphore_wait(ready, 1)

    @pl.when(even)
    def _():
        pass_own(V)
        pass_own(K)

    for at, (a, j) in enumerate(ORDER[:6]):
        if at > 0:
            wait_all(kv_all.at[a, 0, pl.ds(0, len(OTHERS) * ROWS), :], kv_recv.at[a, j])
        if j == SLOTS - 1:
            pass_part(a, j, 0)
            if a == K:
                for part in range(1, PARTS):
                    pass_part(V, j, part)
                    pass_part(K, j, part)
        else:
            for dx, dc in ARRIVAL:
                source = partner(s, dx, dc)
                if at == 0:
                    kv_copy(a, j, s, source).wait_recv()
                pass_after(a, j, source)
                pass_before(a, j, source)
        if at + AHEAD < len(ORDER):
            send(*ORDER[at + AHEAD])

    @pl.when(jnp.logical_not(has_before))
    def _():
        kv_all[:, :, pl.ds(0, HALO), :] = jnp.zeros((2, SLOTS, HALO, HD), BF16)

    @pl.when(jnp.logical_not(has_after))
    def _():
        kv_all[:, :, pl.ds(HALO + GROUP, HALO), :] = jnp.zeros((2, SLOTS, HALO, HD), BF16)

    lane = lax.broadcasted_iota(jnp.int32, (8, HD), 1)
    ints[...] = jnp.zeros_like(ints)
    ints[0, :, :SAMPLES] = jnp.broadcast_to(image_buf[...] + TXT, (8, SAMPLES))
    ints[1, :, :SAMPLES] = jnp.broadcast_to(text_buf[...], (8, SAMPLES))
    lengths = ints[0]
    ends = lengths
    step = 1
    while step < SAMPLES:
        ends = ends + jnp.where(lane >= step, pltpu.roll(ends, step, 1), 0)
        step *= 2
    starts = (ends - lengths)[:1]
    ends = ends[:1]
    text_ends = starts + ints[1][:1]

    def mark(i, carry):
        first = pl.multiple_of(i * 64, 64)
        position = dp * GROUP - HALO + first + lax.broadcasted_iota(jnp.int32, (64, HD), 0)
        inside = (position >= starts) & (position < ends)
        usable = inside & ((position >= starts + TXT) | (position < text_ends))
        mark_k[pl.ds(first, 64), :] = jnp.where(usable, MARK_K, 0.0).astype(BF16)

        @pl.when((i >= HALO // 64) & (i < (HALO + GROUP) // 64))
        def _():
            mark_q[pl.ds(pl.multiple_of(first - HALO, 64), 64), :] = jnp.where(inside, MARK_Q, 0.0).astype(BF16)

        return carry

    lax.fori_loop(0, EXT // 64, mark, 0)

    own_rows = block(s * ROWS)
    own_ext = block(HALO + s * ROWS)
    wait_all(kv_all.at[K, :, own_ext, :], own_sem.at[0])
    wait_all(kv_all.at[V, :, own_ext, :], own_sem.at[1])
    wait_all(q_all.at[:, own_rows, :], own_sem.at[2])
    for j in range(SLOTS - 1):
        attend_whole(j)
    attend_steps(SLOTS - 1)

    sent = k_src.at[:, pl.ds(0, len(OTHERS) * SLOTS * HD)]
    for i in range(3):
        wait_all(sent, x_send.at[i])

    @pl.when(has_after)
    def _():
        wait_all(kv_all.at[:, :, pl.ds(0, HALO), :], z_send.at[0])

    @pl.when(has_before)
    def _():
        wait_all(kv_all.at[:, :, pl.ds(0, HALO), :], z_send.at[1])

    wait_all(o_buf.at[:, own_rows, :], own_sem.at[3])
    for j in range(SLOTS):
        wait_all(out.at[:, pl.ds(0, len(OTHERS) * HD)], out_recv.at[j])
    wait_all(sent, x_send.at[3])


def solution(mesh):
    groups = mesh.shape["dp"]
    dma = pltpu.SemaphoreType.DMA

    def local(q_in, k_in, v_in, q_gain, k_gain, image_tokens, text_tokens):
        rows, width = q_in.shape
        operands = (
            q_in, k_in, v_in,
            q_gain.reshape(1, HD), k_gain.reshape(1, HD),
            image_tokens.reshape(1, SAMPLES), text_tokens.reshape(1, SAMPLES),
        )
        return pl.pallas_call(
            functools.partial(kernel, groups),
            out_shape=jax.ShapeDtypeStruct((rows, width), BF16),
            in_specs=[pl.BlockSpec(memory_space=pltpu.HBM)] * 7,
            out_specs=pl.BlockSpec(memory_space=pl.ANY),
            scratch_shapes=[
                pltpu.VMEM((rows, width), BF16),
                pltpu.VMEM((rows, width), BF16),
                pltpu.VMEM((rows, width), BF16),
                pltpu.VMEM((rows, width), BF16),
                pltpu.VMEM((2, SLOTS, EXT, HD), BF16),
                pltpu.VMEM((SLOTS, GROUP, HD), BF16),
                pltpu.VMEM((SLOTS, GROUP, HD), BF16),
                pltpu.VMEM((GROUP, HD), BF16),
                pltpu.VMEM((EXT, HD), BF16),
                pltpu.VMEM((2, 1, HD), F32),
                pltpu.VMEM((1, SAMPLES), jnp.int32),
                pltpu.VMEM((1, SAMPLES), jnp.int32),
                pltpu.VMEM((2, 8, HD), jnp.int32),
                dma((6,)),
                dma((4,)),
                pltpu.SemaphoreType.REGULAR,
                dma((4,)),
                dma((2,)),
                dma((SEQ,)),
                dma((2, SLOTS)),
                dma((SLOTS,)),
                dma((PARTS, SLOTS)),
                dma((PARTS, SLOTS)),
                dma((SLOTS,)),
            ],
            compiler_params=pltpu.CompilerParams(
                collective_id=0, has_side_effects=True, vmem_limit_bytes=VMEM_BYTES
            ),
            cost_estimate=pl.CostEstimate(flops=4_000_000_000, bytes_accessed=4_000_000, transcendentals=5_000_000),
            name="joint_attention",
        )(*[pltpu.with_memory_space_constraint(operand, pltpu.HBM) for operand in operands])

    split = P(("dp", "seq"), None)
    return jax.shard_map(
        local,
        mesh=mesh,
        in_specs=(split, split, split, P(), P(), P(), P()),
        out_specs=split,
        check_vma=False,
    )
```

```python
import functools

import jax
import jax.numpy as jnp
from jax import lax
from jax.experimental import pallas as pl
from jax.experimental.pallas import tpu as pltpu
from jax.sharding import PartitionSpec as P

MESH = pl.DeviceIdType.MESH
BF16 = jnp.bfloat16
F32 = jnp.float32

HD = 128
TXT = 128
EPS = 1e-06
SEQ = 8
SLOTS = 3
ROWS = 128
GROUP = SEQ * ROWS
HALO = 704
EXT = GROUP + 2 * HALO
BLOCK = 256
WINDOW = BLOCK + 2 * HALO
SAMPLES = 64
VMEM_BYTES = 48 * 1024 * 1024
NORM_HEADS = 12
K, V, Q = 0, 1, 2
PARTS = 3
ORDER = ((V, 0), (K, 0), (V, 1), (K, 1), (V, 2), (K, 2), (Q, 0), (Q, 1), (Q, 2))
AHEAD = 4

MARK_Q = 64.0
MARK_K = 128.0
SCALE = 1.4426950408889634 / HD**0.5

OTHERS = ((1, 0), (-1, 0), (2, 0), (1, 1), (-1, 1), (2, 1), (0, 1))
ARRIVAL = ((0, 1), (1, 0), (-1, 0), (1, 1), (-1, 1), (2, 0), (2, 1))
NT = (((1,), (1,)), ((), ()))


def partner(s, dx, dc):
    return lax.rem(s // 2 + dx + 4, 4) * 2 + lax.rem(s % 2 + dc, 2)


def kernel(
    groups,
    q_in, k_in, v_in, q_gain, k_gain, image, text,
    out,
    q_buf, k_buf, q_src, k_src, kv_all, q_all, o_buf, mark_q, mark_k, gains, image_buf, text_buf, ints,
    load_sem, own_sem, ready, x_send, z_send, v_recv, kv_recv, q_recv, halo_left, halo_right, out_recv,
):
    dp = lax.axis_index("dp")
    s = lax.axis_index("seq")
    has_after = dp < groups - 1
    has_before = dp > 0
    odd = lax.rem(dp, 2) == 1
    even = jnp.logical_not(odd)
    after = lax.rem(dp + 1, groups)
    before = lax.rem(dp + groups - 1, groups)

    barrier = pltpu.get_barrier_semaphore()
    for dx, dc in OTHERS:
        pl.semaphore_signal(barrier, 1, device_id=(dp, partner(s, dx, dc)), device_id_type=MESH)

    @pl.when(even & has_after)
    def _():
        pl.semaphore_signal(barrier, 1, device_id=(after, s), device_id_type=MESH)

    @pl.when(even & has_before)
    def _():
        pl.semaphore_signal(barrier, 1, device_id=(before, s), device_id_type=MESH)

    small = [
        pltpu.make_async_copy(src, dst, load_sem.at[i])
        for i, (src, dst) in enumerate(
            ((k_gain, gains.at[0]), (q_gain, gains.at[1]), (image, image_buf), (text, text_buf))
        )
    ]
    load_k = pltpu.make_async_copy(k_in, k_buf, load_sem.at[4])
    load_q = pltpu.make_async_copy(q_in, q_buf, load_sem.at[5])
    load_k.start()
    for copy in small:
        copy.start()
    load_q.start()

    def cols(head, count=1):
        return pl.ds(pl.multiple_of(head * HD, HD), count * HD)

    def block(first, count=ROWS):
        return pl.ds(pl.multiple_of(first, 64), count)

    def remote(src, dst, send, recv, dev):
        return pltpu.make_async_remote_copy(
            src_ref=src, dst_ref=dst, send_sem=send, recv_sem=recv, device_id=dev, device_id_type=MESH
        )

    def wait_all(ref, sem):
        pltpu.make_async_copy(ref, ref, sem).wait()

    def source_of(a):
        return k_src if a == K else v_in

    def kv_copy(a, j, to, source):
        recv = v_recv.at[source] if (a, j) == (V, 0) else kv_recv.at[a, j]
        return remote(
            source_of(a).at[:, cols(to * SLOTS + j)], kv_all.at[a, j, block(HALO + source * ROWS), :],
            x_send.at[a], recv, (dp, to),
        )

    def q_copy(j, to, source):
        return remote(
            q_src.at[:, cols(to * SLOTS + j)], q_all.at[j, block(source * ROWS), :],
            x_send.at[2], q_recv.at[j], (dp, to),
        )

    def out_copy(j, to, source):
        return remote(
            o_buf.at[j, block(to * ROWS), :], out.at[:, cols(source * SLOTS + j)],
            x_send.at[3], out_recv.at[j], (dp, to),
        )

    def halo_rows(a, j, source, first, count, own):
        if own:
            return source_of(a).at[pl.ds(first, count), cols(s * SLOTS + j)]
        return kv_all.at[a, j, block(HALO + source * ROWS + first, count), :]

    def pass_after(a, j, source, own=False):
        def start(first):
            remote(
                halo_rows(a, j, source, first, ROWS - first, own),
                kv_all.at[a, j, block(source * ROWS + first - (GROUP - HALO), ROWS - first), :],
                z_send.at[0], halo_left.at[(SEQ - 1 - source) // 2, j], (after, s),
            ).start()

        @pl.when((source >= 3) & has_after)
        def _():
            start(0)

        @pl.when((source == 2) & has_after)
        def _():
            start(64)

    def pass_before(a, j, source, own=False):
        def start(count):
            remote(
                halo_rows(a, j, source, 0, count, own),
                kv_all.at[a, j, block(HALO + GROUP + source * ROWS, count), :],
                z_send.at[1], halo_right.at[source // 2, j], (before, s),
            ).start()

        @pl.when((source <= 4) & has_before)
        def _():
            start(ROWS)

        @pl.when((source == 5) & has_before)
        def _():
            start(64)

    def pass_own(a):
        for j in range(SLOTS):
            pass_after(a, j, s, own=True)
            pass_before(a, j, s, own=True)

    def pass_part(a, j, part):
        for source in (2 * part, 2 * part + 1):
            mirror = SEQ - 1 - source

            @pl.when(mirror != s)
            def _():
                pass_after(a, j, mirror)

            @pl.when(source != s)
            def _():
                pass_before(a, j, source)

    def own_kv(a, j):
        return pltpu.make_async_copy(
            source_of(a).at[:, cols(s * SLOTS + j)], kv_all.at[a, j, block(HALO + s * ROWS), :], own_sem.at[a]
        )

    def own_q(j):
        return pltpu.make_async_copy(
            q_src.at[:, cols(s * SLOTS + j)], q_all.at[j, block(s * ROWS), :], own_sem.at[2]
        )

    def own_out(j):
        return pltpu.make_async_copy(
            o_buf.at[j, block(s * ROWS), :], out.at[:, cols(s * SLOTS + j)], own_sem.at[3]
        )

    def normalize(buf, gain, to):
        def some(i, carry):
            for u in range(NORM_HEADS):
                where = cols(i * NORM_HEADS + u)
                x = buf[:, where].astype(F32)
                square = jnp.sum(x * x, axis=1, keepdims=True) * (1.0 / HD)
                to[:, where] = (x * lax.rsqrt(square + EPS) * gain).astype(BF16)
            return carry

        lax.fori_loop(0, SEQ * SLOTS // NORM_HEADS, some, 0)

    def wait_halo(sems, part, j, present):
        count = 2 * min(2 * ROWS, HALO - part * 2 * ROWS)

        @pl.when(present)
        def _():
            wait_all(kv_all.at[K, 0, pl.ds(0, count), :], sems.at[part, j])

    def weigh(j, rows, keys):
        q = jnp.concatenate([q_all[j, rows, :], mark_q[rows, :]], axis=1)
        k = jnp.concatenate([kv_all[K, j, keys, :], mark_k[keys, :]], axis=1)
        v = kv_all[V, j, keys, :]
        scores = lax.dot_general(q, k, NT, preferred_element_type=F32)
        top = jnp.max(scores, axis=1, keepdims=True)
        weights = jnp.exp2((scores - top) * SCALE).astype(BF16)
        return top, jnp.dot(weights, jnp.concatenate([v, jnp.ones_like(v)], axis=1), preferred_element_type=F32)

    def keep(j, rows, sums):
        o_buf[j, rows, :] = (sums[:, :HD] / sums[:, HD:]).astype(BF16)

    def part_of(first, count):
        return pl.ds(first if isinstance(first, int) else pl.multiple_of(first, HD), count)

    def attend(j, first, blocks):
        for i in range(blocks):
            rows = part_of(first + i * BLOCK, BLOCK)
            keep(j, rows, weigh(j, rows, part_of(first + i * BLOCK, WINDOW))[1])

    def attend_whole(j):
        wait_all(q_all.at[0, pl.ds(0, len(OTHERS) * ROWS), :], q_recv.at[j])
        for part in range(PARTS):
            wait_halo(halo_left, part, j, has_before)
            wait_halo(halo_right, part, j, has_after)
        attend(j, 0, GROUP // BLOCK)
        for dx, dc in OTHERS:
            out_copy(j, partner(s, dx, dc), s).start()
        own_out(j).start()

    def attend_steps(j):
        wait_all(q_all.at[0, pl.ds(0, len(OTHERS) * ROWS), :], q_recv.at[j])
        wait_halo(halo_left, 0, j, has_before)
        wait_halo(halo_right, 0, j, has_after)
        left_late = (s < SEQ // 2) | ((s < 6) & (lax.rem(dp, 8) == 0) & has_before)
        right_late = jnp.logical_not(left_late)

        def send_rows(first, count):
            for i in range(count // ROWS):
                to = first // ROWS + i

                @pl.when(to != s)
                def _():
                    out_copy(j, to, s).start()

                @pl.when(to == s)
                def _():
                    own_out(j).start()

        for part in range(1, PARTS):
            wait_halo(halo_right, part, j, left_late & has_after)
            wait_halo(halo_left, part, j, right_late & has_before)
        half = jnp.where(left_late, 2 * BLOCK, 0)
        attend(j, half, 2)
        send_rows(half, 2 * BLOCK)

        wait_halo(halo_left, 1, j, left_late & has_before)
        wait_halo(halo_right, 1, j, right_late & has_after)
        middle = jnp.where(left_late, BLOCK, 2 * BLOCK)
        edge = part_of(jnp.where(left_late, 0, 3 * BLOCK), BLOCK)
        attend(j, middle, 1)
        top_near, sums_near = weigh(j, edge, part_of(jnp.where(left_late, BLOCK, 3 * BLOCK), WINDOW - BLOCK))
        send_rows(middle, BLOCK)

        wait_halo(halo_left, 2, j, left_late & has_before)
        wait_halo(halo_right, 2, j, right_late & has_after)
        top_far, sums_far = weigh(j, edge, part_of(jnp.where(left_late, 0, EXT - BLOCK), BLOCK))
        top = jnp.maximum(top_near, top_far)
        near, far = jnp.exp2((top_near - top) * SCALE), jnp.exp2((top_far - top) * SCALE)
        keep(j, edge, sums_near * near + sums_far * far)
        send_rows(jnp.where(left_late, 0, 3 * BLOCK), BLOCK)

    @pl.when(even)
    def _():
        pl.semaphore_wait(barrier, len(OTHERS))

    @pl.when(odd & has_after)
    def _():
        pl.semaphore_wait(barrier, len(OTHERS) + 2)

    @pl.when(odd & jnp.logical_not(has_after))
    def _():
        pl.semaphore_wait(barrier, len(OTHERS) + 1)

    def send(a, j):
        for dx, dc in OTHERS:
            to = partner(s, dx, dc)
            (q_copy(j, to, s) if a == Q else kv_copy(a, j, to, s)).start()

    send(V, 0)

    @pl.when(odd)
    def _():
        pl.semaphore_signal(ready, 1, device_id=(before, s), device_id_type=MESH)

    @pl.when(odd & has_after)
    def _():
        pl.semaphore_signal(ready, 1, device_id=(after, s), device_id_type=MESH)

    @pl.when(odd)
    def _():
        pass_own(V)

    load_k.wait()
    for copy in small:
        copy.wait()
    normalize(k_buf, gains[0], k_src)
    send(K, 0)

    @pl.when(odd)
    def _():
        pass_own(K)

    for a, j in ORDER[2:AHEAD]:
        send(a, j)
    for j in range(SLOTS):
        own_kv(K, j).start()
        own_kv(V, j).start()
    load_q.wait()
    normalize(q_buf, gains[1], q_src)
    for j in range(SLOTS):
        own_q(j).start()

    @pl.when(even & has_after & has_before)
    def _():
        pl.semaphore_wait(ready, 2)

    @pl.when(even & jnp.logical_not(has_after & has_before))
    def _():
        pl.semaphore_wait(ready, 1)

    @pl.when(even)
    def _():
        pass_own(V)
        pass_own(K)

    for at, (a, j) in enumerate(ORDER[:6]):
        if at > 0:
            wait_all(kv_all.at[a, 0, pl.ds(0, len(OTHERS) * ROWS), :], kv_recv.at[a, j])
        if j == SLOTS - 1:
            pass_part(a, j, 0)
            if a == K:
                for part in range(1, PARTS):
                    pass_part(V, j, part)
                    pass_part(K, j, part)
        else:
            for dx, dc in ARRIVAL:
                source = partner(s, dx, dc)
                if at == 0:
                    kv_copy(a, j, s, source).wait_recv()
                pass_after(a, j, source)
                pass_before(a, j, source)
        if at + AHEAD < len(ORDER):
            send(*ORDER[at + AHEAD])

    @pl.when(jnp.logical_not(has_before))
    def _():
        kv_all[:, :, pl.ds(0, HALO), :] = jnp.zeros((2, SLOTS, HALO, HD), BF16)

    @pl.when(jnp.logical_not(has_after))
    def _():
        kv_all[:, :, pl.ds(HALO + GROUP, HALO), :] = jnp.zeros((2, SLOTS, HALO, HD), BF16)

    lane = lax.broadcasted_iota(jnp.int32, (8, HD), 1)
    ints[...] = jnp.zeros_like(ints)
    ints[0, :, :SAMPLES] = jnp.broadcast_to(image_buf[...] + TXT, (8, SAMPLES))
    ints[1, :, :SAMPLES] = jnp.broadcast_to(text_buf[...], (8, SAMPLES))
    lengths = ints[0]
    ends = lengths
    step = 1
    while step < SAMPLES:
        ends = ends + jnp.where(lane >= step, pltpu.roll(ends, step, 1), 0)
        step *= 2
    starts = (ends - lengths)[:1]
    ends = ends[:1]
    text_ends = starts + ints[1][:1]

    def mark(i, carry):
        first = pl.multiple_of(i * 64, 64)
        position = dp * GROUP - HALO + first + lax.broadcasted_iota(jnp.int32, (64, HD), 0)
        inside = (position >= starts) & (position < ends)
        usable = inside & ((position >= starts + TXT) | (position < text_ends))
        mark_k[pl.ds(first, 64), :] = jnp.where(usable, MARK_K, 0.0).astype(BF16)

        @pl.when((i >= HALO // 64) & (i < (HALO + GROUP) // 64))
        def _():
            mark_q[pl.ds(pl.multiple_of(first - HALO, 64), 64), :] = jnp.where(inside, MARK_Q, 0.0).astype(BF16)

        return carry

    lax.fori_loop(0, EXT // 64, mark, 0)

    own_rows = block(s * ROWS)
    own_ext = block(HALO + s * ROWS)
    wait_all(kv_all.at[K, :, own_ext, :], own_sem.at[0])
    wait_all(kv_all.at[V, :, own_ext, :], own_sem.at[1])
    wait_all(q_all.at[:, own_rows, :], own_sem.at[2])
    for j in range(SLOTS - 1):
        attend_whole(j)
    attend_steps(SLOTS - 1)

    sent = k_src.at[:, pl.ds(0, len(OTHERS) * SLOTS * HD)]
    for i in range(3):
        wait_all(sent, x_send.at[i])

    @pl.when(has_after)
    def _():
        wait_all(kv_all.at[:, :, pl.ds(0, HALO), :], z_send.at[0])

    @pl.when(has_before)
    def _():
        wait_all(kv_all.at[:, :, pl.ds(0, HALO), :], z_send.at[1])

    wait_all(o_buf.at[:, own_rows, :], own_sem.at[3])
    for j in range(SLOTS):
        wait_all(out.at[:, pl.ds(0, len(OTHERS) * HD)], out_recv.at[j])
    wait_all(sent, x_send.at[3])


def solution(mesh):
    groups = mesh.shape["dp"]
    dma = pltpu.SemaphoreType.DMA

    def local(q_in, k_in, v_in, q_gain, k_gain, image_tokens, text_tokens):
        rows, width = q_in.shape
        operands = (
            q_in, k_in, v_in,
            q_gain.reshape(1, HD), k_gain.reshape(1, HD),
            image_tokens.reshape(1, SAMPLES), text_tokens.reshape(1, SAMPLES),
        )
        return pl.pallas_call(
            functools.partial(kernel, groups),
            out_shape=jax.ShapeDtypeStruct((rows, width), BF16),
            in_specs=[pl.BlockSpec(memory_space=pltpu.HBM)] * 7,
            out_specs=pl.BlockSpec(memory_space=pl.ANY),
            scratch_shapes=[
                pltpu.VMEM((rows, width), BF16),
                pltpu.VMEM((rows, width), BF16),
                pltpu.VMEM((rows, width), BF16),
                pltpu.VMEM((rows, width), BF16),
                pltpu.VMEM((2, SLOTS, EXT, HD), BF16),
                pltpu.VMEM((SLOTS, GROUP, HD), BF16),
                pltpu.VMEM((SLOTS, GROUP, HD), BF16),
                pltpu.VMEM((GROUP, HD), BF16),
                pltpu.VMEM((EXT, HD), BF16),
                pltpu.VMEM((2, 1, HD), F32),
                pltpu.VMEM((1, SAMPLES), jnp.int32),
                pltpu.VMEM((1, SAMPLES), jnp.int32),
                pltpu.VMEM((2, 8, HD), jnp.int32),
                dma((6,)),
                dma((4,)),
                pltpu.SemaphoreType.REGULAR,
                dma((4,)),
                dma((2,)),
                dma((SEQ,)),
                dma((2, SLOTS)),
                dma((SLOTS,)),
                dma((PARTS, SLOTS)),
                dma((PARTS, SLOTS)),
                dma((SLOTS,)),
            ],
            compiler_params=pltpu.CompilerParams(
                collective_id=0, has_side_effects=True, vmem_limit_bytes=VMEM_BYTES
            ),
            cost_estimate=pl.CostEstimate(flops=4_000_000_000, bytes_accessed=4_000_000, transcendentals=5_000_000),
            name="joint_attention",
        )(*[pltpu.with_memory_space_constraint(operand, pltpu.HBM) for operand in operands])

    split = P(("dp", "seq"), None)
    return jax.shard_map(
        local,
        mesh=mesh,
        in_specs=(split, split, split, P(), P(), P(), P()),
        out_specs=split,
        check_vma=False,
    )
```

```python
import functools

import jax
import jax.numpy as jnp
from jax import lax
from jax.experimental import pallas as pl
from jax.experimental.pallas import tpu as pltpu
from jax.sharding import PartitionSpec as P

MESH = pl.DeviceIdType.MESH
BF16 = jnp.bfloat16
F32 = jnp.float32

HD = 128
TXT = 128
EPS = 1e-06
SEQ = 8
SLOTS = 3
ROWS = 128
GROUP = SEQ * ROWS
HALO = 704
EXT = GROUP + 2 * HALO
BLOCK = 256
WINDOW = BLOCK + 2 * HALO
SAMPLES = 64
VMEM_BYTES = 48 * 1024 * 1024
NORM_HEADS = 12
K, V, Q = 0, 1, 2
PARTS = 3
ORDER = ((V, 0), (K, 0), (V, 1), (K, 1), (V, 2), (K, 2), (Q, 0), (Q, 1), (Q, 2))
AHEAD = 4

MARK_Q = 64.0
MARK_K = 128.0
SCALE = 1.4426950408889634 / HD**0.5

OTHERS = ((1, 0), (-1, 0), (2, 0), (1, 1), (-1, 1), (2, 1), (0, 1))
ARRIVAL = ((0, 1), (1, 0), (-1, 0), (1, 1), (-1, 1), (2, 0), (2, 1))
NT = (((1,), (1,)), ((), ()))


def partner(s, dx, dc):
    return lax.rem(s // 2 + dx + 4, 4) * 2 + lax.rem(s % 2 + dc, 2)


def kernel(
    groups,
    q_in, k_in, v_in, q_gain, k_gain, image, text,
    out,
    q_buf, k_buf, q_src, k_src, kv_all, q_all, o_buf, mark_q, mark_k, gains, image_buf, text_buf, ints,
    load_sem, own_sem, ready, x_send, z_send, v_recv, kv_recv, q_recv, halo_left, halo_right, out_recv,
):
    dp = lax.axis_index("dp")
    s = lax.axis_index("seq")
    has_after = dp < groups - 1
    has_before = dp > 0
    odd = lax.rem(dp, 2) == 1
    even = jnp.logical_not(odd)
    after = lax.rem(dp + 1, groups)
    before = lax.rem(dp + groups - 1, groups)

    barrier = pltpu.get_barrier_semaphore()
    for dx, dc in OTHERS:
        pl.semaphore_signal(barrier, 1, device_id=(dp, partner(s, dx, dc)), device_id_type=MESH)

    @pl.when(even & has_after)
    def _():
        pl.semaphore_signal(barrier, 1, device_id=(after, s), device_id_type=MESH)

    @pl.when(even & has_before)
    def _():
        pl.semaphore_signal(barrier, 1, device_id=(before, s), device_id_type=MESH)

    small = [
        pltpu.make_async_copy(src, dst, load_sem.at[i])
        for i, (src, dst) in enumerate(
            ((k_gain, gains.at[0]), (q_gain, gains.at[1]), (image, image_buf), (text, text_buf))
        )
    ]
    load_k = pltpu.make_async_copy(k_in, k_buf, load_sem.at[4])
    load_q = pltpu.make_async_copy(q_in, q_buf, load_sem.at[5])
    load_k.start()
    for copy in small:
        copy.start()
    load_q.start()

    def cols(head, count=1):
        return pl.ds(pl.multiple_of(head * HD, HD), count * HD)

    def block(first, count=ROWS):
        return pl.ds(pl.multiple_of(first, 64), count)

    def remote(src, dst, send, recv, dev):
        return pltpu.make_async_remote_copy(
            src_ref=src, dst_ref=dst, send_sem=send, recv_sem=recv, device_id=dev, device_id_type=MESH
        )

    def wait_all(ref, sem):
        pltpu.make_async_copy(ref, ref, sem).wait()

    def source_of(a):
        return k_src if a == K else v_in

    def kv_copy(a, j, to, source):
        recv = v_recv.at[source] if (a, j) == (V, 0) else kv_recv.at[a, j]
        return remote(
            source_of(a).at[:, cols(to * SLOTS + j)], kv_all.at[a, j, block(HALO + source * ROWS), :],
            x_send, recv, (dp, to),
        )

    def q_copy(j, to, source):
        return remote(
            q_src.at[:, cols(to * SLOTS + j)], q_all.at[j, block(source * ROWS), :],
            x_send, q_recv.at[j], (dp, to),
        )

    def out_copy(j, to, source):
        return remote(
            o_buf.at[j, block(to * ROWS), :], out.at[:, cols(source * SLOTS + j)],
            x_send, out_recv, (dp, to),
        )

    def halo_rows(a, j, source, first, count, own):
        if own:
            return source_of(a).at[pl.ds(first, count), cols(s * SLOTS + j)]
        return kv_all.at[a, j, block(HALO + source * ROWS + first, count), :]

    def halo_index(j, part):
        return j + part if j == SLOTS - 1 else j

    def pass_after(a, j, source, own=False):
        def start(first):
            remote(
                halo_rows(a, j, source, first, ROWS - first, own),
                kv_all.at[a, j, block(source * ROWS + first - (GROUP - HALO), ROWS - first), :],
                z_send.at[0], halo_left.at[halo_index(j, (SEQ - 1 - source) // 2)], (after, s),
            ).start()

        @pl.when((source >= 3) & has_after)
        def _():
            start(0)

        @pl.when((source == 2) & has_after)
        def _():
            start(64)

    def pass_before(a, j, source, own=False):
        def start(count):
            remote(
                halo_rows(a, j, source, 0, count, own),
                kv_all.at[a, j, block(HALO + GROUP + source * ROWS, count), :],
                z_send.at[1], halo_right.at[halo_index(j, source // 2)], (before, s),
            ).start()

        @pl.when((source <= 4) & has_before)
        def _():
            start(ROWS)

        @pl.when((source == 5) & has_before)
        def _():
            start(64)

    def pass_own(a):
        for j in range(SLOTS):
            pass_after(a, j, s, own=True)
            pass_before(a, j, s, own=True)

    def pass_part(a, j, part):
        for source in (2 * part, 2 * part + 1):
            mirror = SEQ - 1 - source

            @pl.when(mirror != s)
            def _():
                pass_after(a, j, mirror)

            @pl.when(source != s)
            def _():
                pass_before(a, j, source)

    def own_kv(a, j):
        return pltpu.make_async_copy(
            source_of(a).at[:, cols(s * SLOTS + j)], kv_all.at[a, j, block(HALO + s * ROWS), :], own_sem.at[0]
        )

    def own_q(j):
        return pltpu.make_async_copy(
            q_src.at[:, cols(s * SLOTS + j)], q_all.at[j, block(s * ROWS), :], own_sem.at[1]
        )

    def own_out(j):
        return pltpu.make_async_copy(
            o_buf.at[j, block(s * ROWS), :], out.at[:, cols(s * SLOTS + j)], own_sem.at[2]
        )

    def normalize(buf, gain, to):
        def some(i, carry):
            for u in range(NORM_HEADS):
                where = cols(i * NORM_HEADS + u)
                x = buf[:, where].astype(F32)
                square = jnp.sum(x * x, axis=1, keepdims=True) * (1.0 / HD)
                to[:, where] = (x * lax.rsqrt(square + EPS) * gain).astype(BF16)
            return carry

        lax.fori_loop(0, SEQ * SLOTS // NORM_HEADS, some, 0)

    def wait_halo(sems, part, j, present):
        count = 2 * min(2 * ROWS, HALO - part * 2 * ROWS) if j == SLOTS - 1 else 2 * HALO

        @pl.when(present)
        def _():
            wait_all(kv_all.at[K, 0, pl.ds(0, count), :], sems.at[halo_index(j, part)])

    def weigh(j, rows, keys):
        q = jnp.concatenate([q_all[j, rows, :], mark_q[rows, :]], axis=1)
        k = jnp.concatenate([kv_all[K, j, keys, :], mark_k[keys, :]], axis=1)
        v = kv_all[V, j, keys, :]
        scores = lax.dot_general(q, k, NT, preferred_element_type=F32)
        top = jnp.max(scores, axis=1, keepdims=True)
        weights = jnp.exp2((scores - top) * SCALE).astype(BF16)
        return top, jnp.dot(weights, jnp.concatenate([v, jnp.ones_like(v)], axis=1), preferred_element_type=F32)

    def keep(j, rows, sums):
        o_buf[j, rows, :] = (sums[:, :HD] / sums[:, HD:]).astype(BF16)

    def part_of(first, count):
        return pl.ds(first if isinstance(first, int) else pl.multiple_of(first, HD), count)

    def attend(j, first, blocks):
        for i in range(blocks):
            rows = part_of(first + i * BLOCK, BLOCK)
            keep(j, rows, weigh(j, rows, part_of(first + i * BLOCK, WINDOW))[1])

    def attend_whole(j):
        wait_all(q_all.at[0, pl.ds(0, len(OTHERS) * ROWS), :], q_recv.at[j])
        wait_halo(halo_left, 0, j, has_before)
        wait_halo(halo_right, 0, j, has_after)
        attend(j, 0, GROUP // BLOCK)
        for dx, dc in OTHERS:
            out_copy(j, partner(s, dx, dc), s).start()
        own_out(j).start()

    def attend_steps(j):
        wait_all(q_all.at[0, pl.ds(0, len(OTHERS) * ROWS), :], q_recv.at[j])
        wait_halo(halo_left, 0, j, has_before)
        wait_halo(halo_right, 0, j, has_after)
        left_late = (s < SEQ // 2) | ((s < 6) & (lax.rem(dp, 8) == 0) & has_before)
        right_late = jnp.logical_not(left_late)

        def send_rows(first, count):
            for i in range(count // ROWS):
                to = first // ROWS + i

                @pl.when(to != s)
                def _():
                    out_copy(j, to, s).start()

                @pl.when(to == s)
                def _():
                    own_out(j).start()

        for part in range(1, PARTS):
            wait_halo(halo_right, part, j, left_late & has_after)
            wait_halo(halo_left, part, j, right_late & has_before)
        half = jnp.where(left_late, 2 * BLOCK, 0)
        attend(j, half, 2)
        send_rows(half, 2 * BLOCK)

        wait_halo(halo_left, 1, j, left_late & has_before)
        wait_halo(halo_right, 1, j, right_late & has_after)
        middle = jnp.where(left_late, BLOCK, 2 * BLOCK)
        edge = part_of(jnp.where(left_late, 0, 3 * BLOCK), BLOCK)
        attend(j, middle, 1)
        top_near, sums_near = weigh(j, edge, part_of(jnp.where(left_late, BLOCK, 3 * BLOCK), WINDOW - BLOCK))
        send_rows(middle, BLOCK)

        wait_halo(halo_left, 2, j, left_late & has_before)
        wait_halo(halo_right, 2, j, right_late & has_after)
        top_far, sums_far = weigh(j, edge, part_of(jnp.where(left_late, 0, EXT - BLOCK), BLOCK))
        top = jnp.maximum(top_near, top_far)
        near, far = jnp.exp2((top_near - top) * SCALE), jnp.exp2((top_far - top) * SCALE)
        keep(j, edge, sums_near * near + sums_far * far)
        send_rows(jnp.where(left_late, 0, 3 * BLOCK), BLOCK)

    @pl.when(even)
    def _():
        pl.semaphore_wait(barrier, len(OTHERS))

    @pl.when(odd & has_after)
    def _():
        pl.semaphore_wait(barrier, len(OTHERS) + 2)

    @pl.when(odd & jnp.logical_not(has_after))
    def _():
        pl.semaphore_wait(barrier, len(OTHERS) + 1)

    def send(a, j):
        for dx, dc in OTHERS:
            to = partner(s, dx, dc)
            (q_copy(j, to, s) if a == Q else kv_copy(a, j, to, s)).start()

    send(V, 0)

    @pl.when(odd)
    def _():
        pl.semaphore_signal(ready, 1, device_id=(before, s), device_id_type=MESH)

    @pl.when(odd & has_after)
    def _():
        pl.semaphore_signal(ready, 1, device_id=(after, s), device_id_type=MESH)

    @pl.when(odd)
    def _():
        pass_own(V)

    load_k.wait()
    for copy in small:
        copy.wait()
    normalize(k_buf, gains[0], k_src)
    send(K, 0)

    @pl.when(odd)
    def _():
        pass_own(K)

    for a, j in ORDER[2:AHEAD]:
        send(a, j)
    for j in range(SLOTS):
        own_kv(K, j).start()
        own_kv(V, j).start()
    load_q.wait()
    normalize(q_buf, gains[1], q_src)
    for j in range(SLOTS):
        own_q(j).start()

    @pl.when(even & has_after & has_before)
    def _():
        pl.semaphore_wait(ready, 2)

    @pl.when(even & jnp.logical_not(has_after & has_before))
    def _():
        pl.semaphore_wait(ready, 1)

    @pl.when(even)
    def _():
        pass_own(V)
        pass_own(K)

    for at, (a, j) in enumerate(ORDER[:6]):
        if at > 0:
            wait_all(kv_all.at[a, 0, pl.ds(0, len(OTHERS) * ROWS), :], kv_recv.at[a, j])
        if j == SLOTS - 1:
            pass_part(a, j, 0)
            if a == K:
                for part in range(1, PARTS):
                    pass_part(V, j, part)
                    pass_part(K, j, part)
        else:
            for dx, dc in ARRIVAL:
                source = partner(s, dx, dc)
                if at == 0:
                    kv_copy(a, j, s, source).wait_recv()
                pass_after(a, j, source)
                pass_before(a, j, source)
        if at + AHEAD < len(ORDER):
            send(*ORDER[at + AHEAD])

    @pl.when(jnp.logical_not(has_before))
    def _():
        kv_all[:, :, pl.ds(0, HALO), :] = jnp.zeros((2, SLOTS, HALO, HD), BF16)

    @pl.when(jnp.logical_not(has_after))
    def _():
        kv_all[:, :, pl.ds(HALO + GROUP, HALO), :] = jnp.zeros((2, SLOTS, HALO, HD), BF16)

    lane = lax.broadcasted_iota(jnp.int32, (8, HD), 1)
    ints[...] = jnp.zeros_like(ints)
    ints[0, :, :SAMPLES] = jnp.broadcast_to(image_buf[...] + TXT, (8, SAMPLES))
    ints[1, :, :SAMPLES] = jnp.broadcast_to(text_buf[...], (8, SAMPLES))
    lengths = ints[0]
    ends = lengths
    step = 1
    while step < SAMPLES:
        ends = ends + jnp.where(lane >= step, pltpu.roll(ends, step, 1), 0)
        step *= 2
    starts = (ends - lengths)[:1]
    ends = ends[:1]
    text_ends = starts + ints[1][:1]

    def mark(i, carry):
        first = pl.multiple_of(i * 64, 64)
        position = dp * GROUP - HALO + first + lax.broadcasted_iota(jnp.int32, (64, HD), 0)
        inside = (position >= starts) & (position < ends)
        usable = inside & ((position >= starts + TXT) | (position < text_ends))
        mark_k[pl.ds(first, 64), :] = jnp.where(usable, MARK_K, 0.0).astype(BF16)

        @pl.when((i >= HALO // 64) & (i < (HALO + GROUP) // 64))
        def _():
            mark_q[pl.ds(pl.multiple_of(first - HALO, 64), 64), :] = jnp.where(inside, MARK_Q, 0.0).astype(BF16)

        return carry

    lax.fori_loop(0, EXT // 64, mark, 0)

    own_rows = block(s * ROWS)
    own_ext = block(HALO + s * ROWS)
    wait_all(kv_all.at[:, :, own_ext, :], own_sem.at[0])
    wait_all(q_all.at[:, own_rows, :], own_sem.at[1])
    for j in range(SLOTS - 1):
        attend_whole(j)
    attend_steps(SLOTS - 1)

    @pl.when(has_after)
    def _():
        wait_all(kv_all.at[:, :, pl.ds(0, HALO), :], z_send.at[0])

    @pl.when(has_before)
    def _():
        wait_all(kv_all.at[:, :, pl.ds(0, HALO), :], z_send.at[1])

    wait_all(o_buf.at[:, own_rows, :], own_sem.at[2])
    wait_all(out.at[:, pl.ds(0, len(OTHERS) * SLOTS * HD)], out_recv)
    wait_all(kv_all.at[:, :, pl.ds(0, 2 * len(OTHERS) * ROWS), :], x_send)


def solution(mesh):
    groups = mesh.shape["dp"]
    dma = pltpu.SemaphoreType.DMA

    def local(q_in, k_in, v_in, q_gain, k_gain, image_tokens, text_tokens):
        rows, width = q_in.shape
        operands = (
            q_in, k_in, v_in,
            q_gain.reshape(1, HD), k_gain.reshape(1, HD),
            image_tokens.reshape(1, SAMPLES), text_tokens.reshape(1, SAMPLES),
        )
        return pl.pallas_call(
            functools.partial(kernel, groups),
            out_shape=jax.ShapeDtypeStruct((rows, width), BF16),
            in_specs=[pl.BlockSpec(memory_space=pltpu.HBM)] * 7,
            out_specs=pl.BlockSpec(memory_space=pl.ANY),
            scratch_shapes=[
                pltpu.VMEM((rows, width), BF16),
                pltpu.VMEM((rows, width), BF16),
                pltpu.VMEM((rows, width), BF16),
                pltpu.VMEM((rows, width), BF16),
                pltpu.VMEM((2, SLOTS, EXT, HD), BF16),
                pltpu.VMEM((SLOTS, GROUP, HD), BF16),
                pltpu.VMEM((SLOTS, GROUP, HD), BF16),
                pltpu.VMEM((GROUP, HD), BF16),
                pltpu.VMEM((EXT, HD), BF16),
                pltpu.VMEM((2, 1, HD), F32),
                pltpu.VMEM((1, SAMPLES), jnp.int32),
                pltpu.VMEM((1, SAMPLES), jnp.int32),
                pltpu.VMEM((2, 8, HD), jnp.int32),
                dma((6,)),
                dma((3,)),
                pltpu.SemaphoreType.REGULAR,
                dma(()),
                dma((2,)),
                dma((SEQ,)),
                dma((2, SLOTS)),
                dma((SLOTS,)),
                dma((SLOTS - 1 + PARTS,)),
                dma((SLOTS - 1 + PARTS,)),
                dma(()),
            ],
            compiler_params=pltpu.CompilerParams(
                collective_id=0, has_side_effects=True, vmem_limit_bytes=VMEM_BYTES
            ),
            cost_estimate=pl.CostEstimate(flops=4_000_000_000, bytes_accessed=4_000_000, transcendentals=5_000_000),
            name="joint_attention",
        )(*[pltpu.with_memory_space_constraint(operand, pltpu.HBM) for operand in operands])

    split = P(("dp", "seq"), None)
    return jax.shard_map(
        local,
        mesh=mesh,
        in_specs=(split, split, split, P(), P(), P(), P()),
        out_specs=split,
        check_vma=False,
    )
```

```python
import functools

import jax
import jax.numpy as jnp
from jax import lax
from jax.experimental import pallas as pl
from jax.experimental.pallas import tpu as pltpu
from jax.sharding import PartitionSpec as P

MESH = pl.DeviceIdType.MESH
BF16 = jnp.bfloat16
F32 = jnp.float32

HD = 128
TXT = 128
EPS = 1e-06
SEQ = 8
SLOTS = 3
ROWS = 128
GROUP = SEQ * ROWS
HALO = 704
EXT = GROUP + 2 * HALO
BLOCK = 256
WINDOW = BLOCK + 2 * HALO
SAMPLES = 64
VMEM_BYTES = 48 * 1024 * 1024
NORM_HEADS = 12
K, V, Q = 0, 1, 2
PARTS = 3
ORDER = ((V, 0), (K, 0), (V, 1), (K, 1), (V, 2), (K, 2), (Q, 0), (Q, 1), (Q, 2))
AHEAD = 4

MARK_Q = 64.0
MARK_K = 128.0
SCALE = 1.4426950408889634 / HD**0.5

OTHERS = ((1, 0), (-1, 0), (2, 0), (1, 1), (-1, 1), (2, 1), (0, 1))
ARRIVAL = ((0, 1), (1, 0), (-1, 0), (1, 1), (-1, 1), (2, 0), (2, 1))
NT = (((1,), (1,)), ((), ()))


def partner(s, dx, dc):
    return lax.rem(s // 2 + dx + 4, 4) * 2 + lax.rem(s % 2 + dc, 2)


def kernel(
    groups,
    q_in, k_in, v_in, q_gain, k_gain, image, text,
    out,
    q_buf, k_buf, q_src, k_src, kv_all, q_all, o_buf, mark_q, mark_k, gains, image_buf, text_buf, ints,
    load_sem, own_sem, ready, x_send, z_send, v_recv, kv_recv, q_recv, halo_left, halo_right, out_recv,
):
    dp = lax.axis_index("dp")
    s = lax.axis_index("seq")
    has_after = dp < groups - 1
    has_before = dp > 0
    odd = lax.rem(dp, 2) == 1
    even = jnp.logical_not(odd)
    after = lax.rem(dp + 1, groups)
    before = lax.rem(dp + groups - 1, groups)

    barrier = pltpu.get_barrier_semaphore()
    for dx, dc in OTHERS:
        pl.semaphore_signal(barrier, 1, device_id=(dp, partner(s, dx, dc)), device_id_type=MESH)

    @pl.when(even & has_after)
    def _():
        pl.semaphore_signal(barrier, 1, device_id=(after, s), device_id_type=MESH)

    @pl.when(even & has_before)
    def _():
        pl.semaphore_signal(barrier, 1, device_id=(before, s), device_id_type=MESH)

    small = [
        pltpu.make_async_copy(src, dst, load_sem.at[i])
        for i, (src, dst) in enumerate(
            ((k_gain, gains.at[0]), (q_gain, gains.at[1]), (image, image_buf), (text, text_buf))
        )
    ]
    load_k = pltpu.make_async_copy(k_in, k_buf, load_sem.at[4])
    load_q = pltpu.make_async_copy(q_in, q_buf, load_sem.at[5])
    load_k.start()
    for copy in small:
        copy.start()
    load_q.start()

    def cols(head, count=1):
        return pl.ds(pl.multiple_of(head * HD, HD), count * HD)

    def block(first, count=ROWS):
        return pl.ds(pl.multiple_of(first, 64), count)

    def remote(src, dst, send, recv, dev):
        return pltpu.make_async_remote_copy(
            src_ref=src, dst_ref=dst, send_sem=send, recv_sem=recv, device_id=dev, device_id_type=MESH
        )

    def wait_all(ref, sem):
        pltpu.make_async_copy(ref, ref, sem).wait()

    def source_of(a):
        return k_src if a == K else v_in

    def kv_copy(a, j, to, source):
        recv = v_recv.at[source] if (a, j) == (V, 0) else kv_recv.at[a, j]
        return remote(
            source_of(a).at[:, cols(to * SLOTS + j)], kv_all.at[a, j, block(HALO + source * ROWS), :],
            x_send, recv, (dp, to),
        )

    def q_copy(j, to, source):
        return remote(
            q_src.at[:, cols(to * SLOTS + j)], q_all.at[j, block(source * ROWS), :],
            x_send, q_recv.at[j], (dp, to),
        )

    def out_copy(j, to, source):
        return remote(
            o_buf.at[j, block(to * ROWS), :], out.at[:, cols(source * SLOTS + j)],
            x_send, out_recv, (dp, to),
        )

    def halo_rows(a, j, source, first, count, own):
        if own:
            return source_of(a).at[pl.ds(first, count), cols(s * SLOTS + j)]
        return kv_all.at[a, j, block(HALO + source * ROWS + first, count), :]

    def halo_index(j, part):
        return j + part if j == SLOTS - 1 else j

    def pass_after(a, j, source, own=False):
        def start(first):
            remote(
                halo_rows(a, j, source, first, ROWS - first, own),
                kv_all.at[a, j, block(source * ROWS + first - (GROUP - HALO), ROWS - first), :],
                z_send.at[0], halo_left.at[halo_index(j, (SEQ - 1 - source) // 2)], (after, s),
            ).start()

        @pl.when((source >= 3) & has_after)
        def _():
            start(0)

        @pl.when((source == 2) & has_after)
        def _():
            start(64)

    def pass_before(a, j, source, own=False):
        def start(count):
            remote(
                halo_rows(a, j, source, 0, count, own),
                kv_all.at[a, j, block(HALO + GROUP + source * ROWS, count), :],
                z_send.at[1], halo_right.at[halo_index(j, source // 2)], (before, s),
            ).start()

        @pl.when((source <= 4) & has_before)
        def _():
            start(ROWS)

        @pl.when((source == 5) & has_before)
        def _():
            start(64)

    def pass_own(a):
        for j in range(SLOTS):
            pass_after(a, j, s, own=True)
            pass_before(a, j, s, own=True)

    def pass_part(a, j, part):
        for source in (2 * part, 2 * part + 1):
            mirror = SEQ - 1 - source

            @pl.when(mirror != s)
            def _():
                pass_after(a, j, mirror)

            @pl.when(source != s)
            def _():
                pass_before(a, j, source)

    def own_kv(a, j):
        return pltpu.make_async_copy(
            source_of(a).at[:, cols(s * SLOTS + j)], kv_all.at[a, j, block(HALO + s * ROWS), :], own_sem.at[0]
        )

    def own_q(j):
        return pltpu.make_async_copy(
            q_src.at[:, cols(s * SLOTS + j)], q_all.at[j, block(s * ROWS), :], own_sem.at[1]
        )

    def own_out(j):
        return pltpu.make_async_copy(
            o_buf.at[j, block(s * ROWS), :], out.at[:, cols(s * SLOTS + j)], own_sem.at[2]
        )

    def normalize(buf, gain, to):
        def some(i, carry):
            for u in range(NORM_HEADS):
                where = cols(i * NORM_HEADS + u)
                x = buf[:, where].astype(F32)
                square = jnp.sum(x * x, axis=1, keepdims=True) * (1.0 / HD)
                to[:, where] = (x * lax.rsqrt(square + EPS) * gain).astype(BF16)
            return carry

        lax.fori_loop(0, SEQ * SLOTS // NORM_HEADS, some, 0)

    def wait_halo(sems, part, j, present):
        count = 2 * min(2 * ROWS, HALO - part * 2 * ROWS) if j == SLOTS - 1 else 2 * HALO

        @pl.when(present)
        def _():
            wait_all(kv_all.at[K, 0, pl.ds(0, count), :], sems.at[halo_index(j, part)])

    def weigh(j, rows, keys):
        q = jnp.concatenate([q_all[j, rows, :], mark_q[rows, :]], axis=1)
        k = jnp.concatenate([kv_all[K, j, keys, :], mark_k[keys, :]], axis=1)
        v = kv_all[V, j, keys, :]
        scores = lax.dot_general(q, k, NT, preferred_element_type=F32)
        top = jnp.max(scores, axis=1, keepdims=True)
        weights = jnp.exp2((scores - top) * SCALE).astype(BF16)
        return top, jnp.dot(weights, jnp.concatenate([v, jnp.ones_like(v)], axis=1), preferred_element_type=F32)

    def keep(j, rows, sums):
        o_buf[j, rows, :] = (sums[:, :HD] / sums[:, HD:]).astype(BF16)

    def part_of(first, count):
        return pl.ds(first if isinstance(first, int) else pl.multiple_of(first, HD), count)

    def attend(j, first, blocks):
        for i in range(blocks):
            rows = part_of(first + i * BLOCK, BLOCK)
            keep(j, rows, weigh(j, rows, part_of(first + i * BLOCK, WINDOW))[1])

    def attend_whole(j):
        wait_all(q_all.at[0, pl.ds(0, len(OTHERS) * ROWS), :], q_recv.at[j])
        wait_halo(halo_left, 0, j, has_before)
        wait_halo(halo_right, 0, j, has_after)
        attend(j, 0, GROUP // BLOCK)
        for dx, dc in OTHERS:
            out_copy(j, partner(s, dx, dc), s).start()
        own_out(j).start()

    def attend_steps(j):
        wait_all(q_all.at[0, pl.ds(0, len(OTHERS) * ROWS), :], q_recv.at[j])
        wait_halo(halo_left, 0, j, has_before)
        wait_halo(halo_right, 0, j, has_after)
        left_late = (s < SEQ // 2) | ((s < 5) & (lax.rem(dp, 8) == 0) & has_before)
        right_late = jnp.logical_not(left_late)

        def send_rows(first, count):
            for i in range(count // ROWS):
                to = first // ROWS + i

                @pl.when(to != s)
                def _():
                    out_copy(j, to, s).start()

                @pl.when(to == s)
                def _():
                    own_out(j).start()

        for part in range(1, PARTS):
            wait_halo(halo_right, part, j, left_late & has_after)
            wait_halo(halo_left, part, j, right_late & has_before)
        half = jnp.where(left_late, 2 * BLOCK, 0)
        attend(j, half, 2)
        send_rows(half, 2 * BLOCK)

        wait_halo(halo_left, 1, j, left_late & has_before)
        wait_halo(halo_right, 1, j, right_late & has_after)
        middle = jnp.where(left_late, BLOCK, 2 * BLOCK)
        edge = part_of(jnp.where(left_late, 0, 3 * BLOCK), BLOCK)
        attend(j, middle, 1)
        top_near, sums_near = weigh(j, edge, part_of(jnp.where(left_late, BLOCK, 3 * BLOCK), WINDOW - BLOCK))
        send_rows(middle, BLOCK)

        wait_halo(halo_left, 2, j, left_late & has_before)
        wait_halo(halo_right, 2, j, right_late & has_after)
        top_far, sums_far = weigh(j, edge, part_of(jnp.where(left_late, 0, EXT - BLOCK), BLOCK))
        top = jnp.maximum(top_near, top_far)
        near, far = jnp.exp2((top_near - top) * SCALE), jnp.exp2((top_far - top) * SCALE)
        keep(j, edge, sums_near * near + sums_far * far)
        send_rows(jnp.where(left_late, 0, 3 * BLOCK), BLOCK)

    @pl.when(even)
    def _():
        pl.semaphore_wait(barrier, len(OTHERS))

    @pl.when(odd & has_after)
    def _():
        pl.semaphore_wait(barrier, len(OTHERS) + 2)

    @pl.when(odd & jnp.logical_not(has_after))
    def _():
        pl.semaphore_wait(barrier, len(OTHERS) + 1)

    def send(a, j):
        for dx, dc in OTHERS:
            to = partner(s, dx, dc)
            (q_copy(j, to, s) if a == Q else kv_copy(a, j, to, s)).start()

    send(V, 0)

    @pl.when(odd)
    def _():
        pl.semaphore_signal(ready, 1, device_id=(before, s), device_id_type=MESH)

    @pl.when(odd & has_after)
    def _():
        pl.semaphore_signal(ready, 1, device_id=(after, s), device_id_type=MESH)

    @pl.when(odd)
    def _():
        pass_own(V)

    load_k.wait()
    for copy in small:
        copy.wait()
    normalize(k_buf, gains[0], k_src)
    send(K, 0)

    @pl.when(odd)
    def _():
        pass_own(K)

    for a, j in ORDER[2:AHEAD]:
        send(a, j)
    for j in range(SLOTS):
        own_kv(K, j).start()
        own_kv(V, j).start()
    load_q.wait()
    normalize(q_buf, gains[1], q_src)
    for j in range(SLOTS):
        own_q(j).start()

    @pl.when(even & has_after & has_before)
    def _():
        pl.semaphore_wait(ready, 2)

    @pl.when(even & jnp.logical_not(has_after & has_before))
    def _():
        pl.semaphore_wait(ready, 1)

    @pl.when(even)
    def _():
        pass_own(V)
        pass_own(K)

    for at, (a, j) in enumerate(ORDER[:6]):
        if at > 0:
            wait_all(kv_all.at[a, 0, pl.ds(0, len(OTHERS) * ROWS), :], kv_recv.at[a, j])
        if j == SLOTS - 1:
            pass_part(a, j, 0)
            if a == K:
                for part in range(1, PARTS):
                    pass_part(V, j, part)
                    pass_part(K, j, part)
        else:
            for dx, dc in ARRIVAL:
                source = partner(s, dx, dc)
                if at == 0:
                    kv_copy(a, j, s, source).wait_recv()
                pass_after(a, j, source)
                pass_before(a, j, source)
        if at + AHEAD < len(ORDER):
            send(*ORDER[at + AHEAD])

    @pl.when(jnp.logical_not(has_before))
    def _():
        kv_all[:, :, pl.ds(0, HALO), :] = jnp.zeros((2, SLOTS, HALO, HD), BF16)

    @pl.when(jnp.logical_not(has_after))
    def _():
        kv_all[:, :, pl.ds(HALO + GROUP, HALO), :] = jnp.zeros((2, SLOTS, HALO, HD), BF16)

    lane = lax.broadcasted_iota(jnp.int32, (8, HD), 1)
    ints[...] = jnp.zeros_like(ints)
    ints[0, :, :SAMPLES] = jnp.broadcast_to(image_buf[...] + TXT, (8, SAMPLES))
    ints[1, :, :SAMPLES] = jnp.broadcast_to(text_buf[...], (8, SAMPLES))
    lengths = ints[0]
    ends = lengths
    step = 1
    while step < SAMPLES:
        ends = ends + jnp.where(lane >= step, pltpu.roll(ends, step, 1), 0)
        step *= 2
    starts = (ends - lengths)[:1]
    ends = ends[:1]
    text_ends = starts + ints[1][:1]

    def mark(i, carry):
        first = pl.multiple_of(i * 64, 64)
        position = dp * GROUP - HALO + first + lax.broadcasted_iota(jnp.int32, (64, HD), 0)
        inside = (position >= starts) & (position < ends)
        usable = inside & ((position >= starts + TXT) | (position < text_ends))
        mark_k[pl.ds(first, 64), :] = jnp.where(usable, MARK_K, 0.0).astype(BF16)

        @pl.when((i >= HALO // 64) & (i < (HALO + GROUP) // 64))
        def _():
            mark_q[pl.ds(pl.multiple_of(first - HALO, 64), 64), :] = jnp.where(inside, MARK_Q, 0.0).astype(BF16)

        return carry

    lax.fori_loop(0, EXT // 64, mark, 0)

    own_rows = block(s * ROWS)
    own_ext = block(HALO + s * ROWS)
    wait_all(kv_all.at[:, :, own_ext, :], own_sem.at[0])
    wait_all(q_all.at[:, own_rows, :], own_sem.at[1])
    for j in range(SLOTS - 1):
        attend_whole(j)
    attend_steps(SLOTS - 1)

    @pl.when(has_after)
    def _():
        wait_all(kv_all.at[:, :, pl.ds(0, HALO), :], z_send.at[0])

    @pl.when(has_before)
    def _():
        wait_all(kv_all.at[:, :, pl.ds(0, HALO), :], z_send.at[1])

    wait_all(o_buf.at[:, own_rows, :], own_sem.at[2])
    wait_all(out.at[:, pl.ds(0, len(OTHERS) * SLOTS * HD)], out_recv)
    wait_all(kv_all.at[:, :, pl.ds(0, 2 * len(OTHERS) * ROWS), :], x_send)


def solution(mesh):
    groups = mesh.shape["dp"]
    dma = pltpu.SemaphoreType.DMA

    def local(q_in, k_in, v_in, q_gain, k_gain, image_tokens, text_tokens):
        rows, width = q_in.shape
        operands = (
            q_in, k_in, v_in,
            q_gain.reshape(1, HD), k_gain.reshape(1, HD),
            image_tokens.reshape(1, SAMPLES), text_tokens.reshape(1, SAMPLES),
        )
        return pl.pallas_call(
            functools.partial(kernel, groups),
            out_shape=jax.ShapeDtypeStruct((rows, width), BF16),
            in_specs=[pl.BlockSpec(memory_space=pltpu.HBM)] * 7,
            out_specs=pl.BlockSpec(memory_space=pl.ANY),
            scratch_shapes=[
                pltpu.VMEM((rows, width), BF16),
                pltpu.VMEM((rows, width), BF16),
                pltpu.VMEM((rows, width), BF16),
                pltpu.VMEM((rows, width), BF16),
                pltpu.VMEM((2, SLOTS, EXT, HD), BF16),
                pltpu.VMEM((SLOTS, GROUP, HD), BF16),
                pltpu.VMEM((SLOTS, GROUP, HD), BF16),
                pltpu.VMEM((GROUP, HD), BF16),
                pltpu.VMEM((EXT, HD), BF16),
                pltpu.VMEM((2, 1, HD), F32),
                pltpu.VMEM((1, SAMPLES), jnp.int32),
                pltpu.VMEM((1, SAMPLES), jnp.int32),
                pltpu.VMEM((2, 8, HD), jnp.int32),
                dma((6,)),
                dma((3,)),
                pltpu.SemaphoreType.REGULAR,
                dma(()),
                dma((2,)),
                dma((SEQ,)),
                dma((2, SLOTS)),
                dma((SLOTS,)),
                dma((SLOTS - 1 + PARTS,)),
                dma((SLOTS - 1 + PARTS,)),
                dma(()),
            ],
            compiler_params=pltpu.CompilerParams(
                collective_id=0, has_side_effects=True, vmem_limit_bytes=VMEM_BYTES
            ),
            cost_estimate=pl.CostEstimate(flops=4_000_000_000, bytes_accessed=4_000_000, transcendentals=5_000_000),
            name="joint_attention",
        )(*[pltpu.with_memory_space_constraint(operand, pltpu.HBM) for operand in operands])

    split = P(("dp", "seq"), None)
    return jax.shard_map(
        local,
        mesh=mesh,
        in_specs=(split, split, split, P(), P(), P(), P()),
        out_specs=split,
        check_vma=False,
    )
```
